256 devices in a mesh: grp: 8 (over y, core), span: 32 (over z, x).
Axes of the slice: x: 4, y: 4, z: 8, core: 2. Of those that a mesh axis runs over, the one named last changes fastest.
Arguments:
- record: float32 [1048576, 128], P(('grp', 'span')), may hold values from -96 to 96, as said below
Outputs:
- triangle: float32 [512, 512], replicated
- operator: float32 [512, 512], replicated
The draws below stay inside these ranges and needn't reach their ends.
Inputs may be any that keep to these rules, and one draw needn't show every extreme that they name: `record`: Real-valued probe samples.
All inputs are finite; a program needn't handle non-finite values.
Results may differ from the reference program's by a relative error of at most 0.0003.
Values sent between devices are 32-bit elements; how exact they have to be, the bound alone decides.
No kernel may reach another device: no remote copies, remote signals or barrier semaphores. Data moves between devices by JAX's collectives and lax.ppermute only.
A program may use at most 64 MiB of HBM per device.

```python
import jax
import jax.numpy as jnp
from jax import lax

COMPS = 128
LAGS = 4
DELAY = 1024
ROWS_DEV = 4096
COLS = 512
SAMPLES = 1048576
HROWS = 1045503


def draw_record(key, part):
    keys = jax.random.split(jax.random.fold_in(key, 17), 5)
    colscale = jnp.exp(jax.random.uniform(keys[0], (1, COMPS), jnp.float32) * 2.302585)
    freq = jax.random.randint(keys[1], (1, COMPS), 1, 32768)
    phase = jax.random.randint(keys[2], (1, COMPS), 0, 65536)
    times = jnp.arange(SAMPLES, dtype=jnp.int32)[:, None]
    turns = (freq * (times % 65536) + phase) % 65536
    wave = 0.8 * jnp.sin(turns.astype(jnp.float32) * (6.2831853 / 65536.0))
    envelope = 0.6 + 1.2 * times.astype(jnp.float32) / SAMPLES
    noise = jax.random.truncated_normal(keys[4], -4.0, 4.0, (SAMPLES, COMPS), jnp.float32)
    return (colscale * envelope * (noise + wave)).astype(jnp.float32)


def setup_inputs(seed: int = 0) -> dict:
    streams_of = jax.random.split(jax.random.key(seed), 2)
    return {
        "record": draw_record(jax.random.fold_in(streams_of[1], 71), 0),
    }


def block_terms(padded, start, count):
    lead = (LAGS - 1) * DELAY + 1
    ext = lax.dynamic_slice_in_dim(padded, start, count + lead, 0)
    hank = jnp.concatenate([ext[k * DELAY:k * DELAY + count + 1] for k in range(LAGS)], 1)
    times = start + jnp.arange(count, dtype=jnp.int32)
    weight = jnp.where(times < HROWS, 1.0, 0.0) - 0.5 * jnp.where(times == 0, 1.0, 0.0) - 0.5 * jnp.where(times == HROWS, 1.0, 0.0)
    weight = weight.astype(jnp.float32)
    inside = jnp.where(times < HROWS, 1.0, 0.0).astype(jnp.float32)
    head = hank[:count]
    gram = lax.dot_general((head * weight[:, None]).astype(jnp.float32), head.astype(jnp.float32), (((0,), (0,)), ((), ())), precision=lax.Precision.HIGHEST, preferred_element_type=jnp.float32)
    cross = lax.dot_general((head * inside[:, None]).astype(jnp.float32), hank[1:count + 1].astype(jnp.float32), (((0,), (0,)), ((), ())), precision=lax.Precision.HIGHEST, preferred_element_type=jnp.float32)
    return (gram, cross)

def reference(record):
    lead = (LAGS - 1) * DELAY + 1
    padded = jnp.concatenate([record, jnp.zeros((lead, COMPS), jnp.float32)], 0)
    blocks = SAMPLES // ROWS_DEV

    def step(carry, index):
        gram, cross = block_terms(padded, (index * ROWS_DEV).astype(jnp.int32), ROWS_DEV)
        return ((carry[0] + gram, carry[1] + cross), None)
    zeros = jnp.zeros((COLS, COLS), jnp.float32)
    (gram, cross), unused = lax.scan(step, (zeros, zeros), jnp.arange(blocks, dtype=jnp.int32))
    lower = jnp.linalg.cholesky(gram / HROWS)
    middle = jax.scipy.linalg.solve_triangular(lower, cross / HROWS, lower=True)
    operator = jax.scipy.linalg.solve_triangular(lower, middle.T, lower=True).T
    return (lower.T, operator)
```

```python
import functools

import jax
import jax.numpy as jnp
from jax import lax
from jax.experimental import pallas as pl
from jax.experimental.pallas import tpu as pltpu
from jax.sharding import PartitionSpec as P

LAGS = 4
DELAY = 1024
N = 128
COLS = LAGS * N
HALF = DELAY // 2
SPAN = DELAY + HALF
AXES = ("grp", "span")
HIGHEST = lax.Precision.HIGHEST
VMEM_LIMIT = 48 * 2**20

PAIRS = [(i, j) for i in range(LAGS) for j in range(i, LAGS)]
GRAM = {pair: index for index, pair in enumerate(PAIRS)}
CROSS = {(i, j): len(PAIRS) + LAGS * i + j for i in range(LAGS) for j in range(LAGS)}
BLOCKS = len(GRAM) + len(CROSS)


def exact(left, right, dims):
    return lax.dot_general(left, right, (dims, ((), ())), precision=HIGHEST, preferred_element_type=jnp.float32)


def rows_product(left, right):
    return lax.dot_general(left, right, (((0,), (0,)), ((), ())), preferred_element_type=jnp.float32)


def parts(value):
    high = value.astype(jnp.bfloat16)
    low = (value - high.astype(jnp.float32)).astype(jnp.bfloat16)
    return jnp.concatenate([high, low], 1)


def fold(value):
    return (value[:N, :N] + value[N:, :N]) + (value[:N, N:] + value[N:, N:])


def lag_products(left, right, zero_lag=False):
    first = rows_product(left, right[:, : 2 * N])
    same, back = fold(first[: 2 * N]), fold(first[2 * N :])
    ahead = None if zero_lag else fold(rows_product(left[:, : 2 * N], right[:, 2 * N :]))
    return same, back, ahead


def local_kernel(edge_ref, rec_ref, out_ref, split_ref, same_ref, back_ref, ahead_ref):
    count = rec_ref.shape[0]
    for q in range(LAGS):
        lo, hi = q * DELAY, (q + 1) * DELAY
        split_ref[lo:hi, : 2 * N] = parts(rec_ref[lo:hi, :])
        if q < LAGS - 1:
            following = rec_ref[lo + 1 : hi + 1, :]
        else:
            following = jnp.concatenate([rec_ref[lo + 1 : hi, :], jnp.zeros((1, N), jnp.float32)], 0)
        split_ref[lo:hi, 2 * N :] = parts(following)
    for q in range(LAGS):
        left = split_ref[q * DELAY : (q + 1) * DELAY, :]
        for d in range(LAGS - q):
            right = split_ref[(q + d) * DELAY : (q + d + 1) * DELAY, :]
            same, back, ahead = lag_products(left, right, d == 0)
            same_ref[LAGS * q + d] = same
            back_ref[LAGS * q + d] = back
            if d:
                ahead_ref[LAGS * q + d] = ahead
    first, last = edge_ref[0], edge_ref[1]

    def kept(q, m):
        if q < m:
            return (1 - first).astype(jnp.float32)
        if q > m:
            return (1 - last).astype(jnp.float32)
        return None

    def total(ref, d, m):
        value = None
        for q in range(LAGS - d):
            factor, term = kept(q, m), ref[LAGS * q + d]
            term = term if factor is None else term * factor
            value = term if value is None else value + term
        return value

    for i, j in PAIRS:
        d = j - i
        out_ref[GRAM[i, j]] = total(same_ref, d, i)
        out_ref[CROSS[j, i]] = total(back_ref, d, i)
        if d:
            out_ref[CROSS[i, j]] = total(ahead_ref, d, i)

    @pl.when(first + last > 0)
    def _():
        def wide(offset, steps):
            pieces = [rec_ref[offset + k * DELAY : offset + k * DELAY + 1, :] for k in range(steps)]
            pieces += [jnp.zeros((1, N), jnp.float32)] * (LAGS - steps)
            return jnp.concatenate(pieces, 1)

        start = wide(0, LAGS) * first.astype(jnp.float32)
        final = wide(DELAY - 1, LAGS) * last.astype(jnp.float32)
        after = wide(DELAY, LAGS - 1)
        blank = jnp.zeros((6, COLS), jnp.float32)
        ends = jnp.concatenate([start, final, blank], 0)
        steps = jnp.concatenate([jnp.zeros((1, COLS), jnp.float32), after, blank], 0)
        outer = ((0,), (0,))
        for i in range(LAGS):
            for j in range(LAGS):
                a, b = ends[:, i * N : (i + 1) * N], ends[:, j * N : (j + 1) * N]
                c = steps[:, j * N : (j + 1) * N]
                if j >= i:
                    out_ref[GRAM[i, j]] -= 0.5 * exact(a, b, outer)
                out_ref[CROSS[i, j]] -= exact(c, a, outer) if i >= j else exact(a, c, outer)


def halo_kernel(edge_ref, acc_ref, split_ref, down_ref, up_ref, out_ref, below, above):
    below[:, : 2 * N] = parts(down_ref[:SPAN, :])
    below[:, 2 * N :] = parts(down_ref[1 : SPAN + 1, :])
    above[:, : 2 * N] = parts(up_ref[...])
    own = split_ref[0:16, : 2 * N].astype(jnp.float32)[0:1]
    own = (own[:, :N] + own[:, N:]) * (1 - edge_ref[0]).astype(jnp.float32)
    above[:, 2 * N :] = parts(jnp.concatenate([up_ref[1:SPAN, :], own], 0))

    def own_rows(start, size):
        return split_ref[start : start + size, :]

    pairs = {
        1: [(own_rows(3 * DELAY, DELAY), below[:DELAY, :])],
        2: [(own_rows(2 * DELAY, DELAY), below[:DELAY, :]), (above[HALF:, :], own_rows(DELAY, DELAY))],
        3: [
            (own_rows(DELAY, DELAY), below[:DELAY, :]),
            (above[HALF:, :], own_rows(2 * DELAY, DELAY)),
            (own_rows(2 * DELAY, HALF), below[DELAY:, :]),
            (above[:HALF, :], own_rows(DELAY + HALF, HALF)),
        ],
    }
    lastrow = lax.broadcasted_iota(jnp.int32, (16, N), 0) == 15
    entering = parts(jnp.where(lastrow, jnp.broadcast_to(down_ref[0:1, :], (16, N)), 0.0))
    count = LAGS * DELAY
    fix = fold(rows_product(entering, split_ref[count - 16 : count, : 2 * N]))
    for i in range(LAGS):
        out_ref[GRAM[i, i]] = acc_ref[GRAM[i, i]]
        out_ref[CROSS[i, i]] = acc_ref[CROSS[i, i]] + fix
    for d in range(1, LAGS):
        stop = (LAGS - d) * DELAY
        same = None
        back = fold(rows_product(entering, below[DELAY - 16 : DELAY, : 2 * N])) if d == 1 else None
        ahead = fold(rows_product(split_ref[stop - 16 : stop, : 2 * N], entering))
        for left, right in pairs[d]:
            s, b, a = lag_products(left, right)
            same = s if same is None else same + s
            back = b if back is None else back + b
            ahead = ahead + a
        for i in range(LAGS - d):
            j = i + d
            out_ref[GRAM[i, j]] = acc_ref[GRAM[i, j]] + same
            out_ref[CROSS[j, i]] = acc_ref[CROSS[j, i]] + back
            out_ref[CROSS[i, j]] = acc_ref[CROSS[i, j]] + ahead


def lanes(value, j):
    return jnp.broadcast_to(value[:, j : j + 1], (value.shape[0], N))


def line(value, t, n):
    return jnp.broadcast_to(value[t : t + 1, :], (n, N))


def factor(rest, inverse):
    sub = lax.broadcasted_iota(jnp.int32, (8, N), 0)
    lane = lax.broadcasted_iota(jnp.int32, (8, N), 1)
    uppers, inverses = [], []
    for k in range(N // 8):
        n = rest.shape[0] - 8
        top, top_inverse = rest[:8], inverse[:8]
        cols = [lanes(top, 8 * k + t) for t in range(8)]
        if n:
            rest, inverse = rest[8:], inverse[8:]
            below = [lanes(rest, 8 * k + t) for t in range(8)]
        pivots = jnp.zeros((8, N), jnp.float32)
        for t in range(8):
            pivot = line(cols[t], t, 8)
            recip = 1.0 / pivot
            mult = jnp.where(sub > t, cols[t] * recip, 0.0)
            if n:
                mult_below = below[t] * jnp.broadcast_to(recip[:1], (n, N))
            for u in range(t + 1, 8):
                entry = cols[u][t : t + 1, :]
                if n:
                    below[u] = below[u] - mult_below * jnp.broadcast_to(entry, (n, N))
                cols[u] = cols[u] - mult * jnp.broadcast_to(entry, (8, N))
            pivots = jnp.where(sub == t, pivot, pivots)
            if n:
                rest = rest - mult_below * line(top, t, n)
                inverse = inverse - mult_below * line(top_inverse, t, n)
            top = top - mult * line(top, t, 8)
            top_inverse = top_inverse - mult * line(top_inverse, t, 8)
        root = lax.rsqrt(pivots)
        uppers.append(jnp.where(lane >= sub + 8 * k, top * root, 0.0))
        inverses.append(top_inverse * root)
    return jnp.concatenate(uppers, 0), jnp.concatenate(inverses, 0)


def tail_kernel(scale, sum_ref, tri_ref, op_ref, work, right, inv):
    for i in range(LAGS):
        for j in range(LAGS):
            if j >= i:
                work[i, :, j * N : (j + 1) * N] = sum_ref[GRAM[i, j]] * scale
            block = sum_ref[CROSS[i, j]]
            work[i, :, COLS + j * N : COLS + (j + 1) * N] = (block.T if i >= j else block) * scale
    rows = lax.broadcasted_iota(jnp.int32, (N, N), 0)
    eye = jnp.where(rows == lax.broadcasted_iota(jnp.int32, (N, N), 1), 1.0, 0.0).astype(jnp.float32)
    for k in range(LAGS):
        for j in range(k):
            tri_ref[k * N : (k + 1) * N, j * N : (j + 1) * N] = jnp.zeros((N, N), jnp.float32)

    def finish(k, upper, inverse):
        tri_ref[k * N : (k + 1) * N, k * N : (k + 1) * N] = upper
        solved = exact(inverse, work[k, :, (k + 1) * N :], ((1,), (0,)))
        work[k, :, (k + 1) * N :] = solved
        if k < LAGS - 1:
            tri_ref[k * N : (k + 1) * N, (k + 1) * N :] = solved[:, : (LAGS - 1 - k) * N]
        for i in range(k + 1, LAGS):
            lo = (i - k - 1) * N
            work[i, :, i * N :] = work[i, :, i * N :] - exact(solved[:, lo : lo + N], solved[:, lo:], ((0,), (0,)))

    def step(k, carry):
        upper, inverse = factor(work[k, :, pl.ds(pl.multiple_of(k * N, N), N)], eye)
        inv[k] = inverse
        for which in range(LAGS):
            pl.when(k == which)(functools.partial(finish, which, upper, inverse))
        return carry

    lax.fori_loop(0, LAGS, step, 0)
    for i in range(LAGS):
        right[i * N : (i + 1) * N, :] = work[i, :, COLS:]
    for j in range(LAGS):
        lo, hi = j * N, (j + 1) * N
        solved = exact(right[:, lo:hi], inv[j], ((1,), (1,)))
        op_ref[:, lo:hi] = solved
        if j < LAGS - 1:
            right[:, hi:] = right[:, hi:] - exact(solved, tri_ref[lo:hi, hi:], ((1,), (0,)))


def shifted(value, steps):
    count = lax.axis_size(AXES)
    leading, last = (max(0, -steps), min(count, count - steps))
    return lax.ppermute(value, AXES, [(source, source + steps) for source in range(leading, last)])


def spread_sum(value):
    pieces = lax.psum(tuple(value[r : r + 32] for r in range(0, value.shape[0], 32)), AXES)
    return jnp.concatenate(pieces, 0)


def averaged_blocks(record):
    count = record.shape[0]
    devices = lax.axis_size(AXES)
    index = lax.axis_index(AXES)
    edge = jnp.stack([index == 0, index == devices - 1]).astype(jnp.int32)
    down = shifted(record[: SPAN + 8], -1)
    up = shifted(record[count - SPAN :], 1)
    smem, vmem = pl.BlockSpec(memory_space=pltpu.SMEM), pl.BlockSpec(memory_space=pltpu.VMEM)
    params = pltpu.CompilerParams(vmem_limit_bytes=VMEM_LIMIT)
    block = jax.ShapeDtypeStruct((BLOCKS, N, N), jnp.float32)
    local, split = pl.pallas_call(
        local_kernel,
        out_shape=[block, jax.ShapeDtypeStruct((count, 4 * N), jnp.bfloat16)],
        in_specs=[smem, vmem],
        out_specs=[vmem, vmem],
        scratch_shapes=[pltpu.VMEM((LAGS * LAGS, N, N), jnp.float32)] * 3,
        compiler_params=params,
        cost_estimate=pl.CostEstimate(flops=4 * 10**9, bytes_accessed=8 * 2**20, transcendentals=0),
        name="local_products",
    )(edge, record)
    summed = pl.pallas_call(
        halo_kernel,
        out_shape=block,
        in_specs=[smem, vmem, vmem, vmem, vmem],
        out_specs=vmem,
        scratch_shapes=[pltpu.VMEM((SPAN, 4 * N), jnp.bfloat16)] * 2,
        compiler_params=params,
        cost_estimate=pl.CostEstimate(flops=3 * 10**9, bytes_accessed=9 * 2**20, transcendentals=0),
        name="halo_products",
    )(edge, local, split, down, up)
    return spread_sum(summed.reshape(BLOCKS * N, N)).reshape(BLOCKS, N, N)


def on_device(record):
    last_row = record.shape[0] * lax.axis_size(AXES) - (LAGS - 1) * DELAY - 1
    total = averaged_blocks(record)
    vmem = pl.BlockSpec(memory_space=pltpu.VMEM)
    square = jax.ShapeDtypeStruct((COLS, COLS), jnp.float32)
    return tuple(
        pl.pallas_call(
            functools.partial(tail_kernel, 1.0 / last_row),
            out_shape=[square, square],
            in_specs=[vmem],
            out_specs=[vmem, vmem],
            scratch_shapes=[
                pltpu.VMEM((LAGS, N, 2 * COLS), jnp.float32),
                pltpu.VMEM((COLS, COLS), jnp.float32),
                pltpu.VMEM((LAGS, N, N), jnp.float32),
            ],
            compiler_params=pltpu.CompilerParams(vmem_limit_bytes=VMEM_LIMIT),
            name="factor_and_solve",
        )(total)
    )


def solution(mesh):
    placed = (P(AXES, None),)
    return jax.shard_map(on_device, mesh=mesh, in_specs=placed, out_specs=(P(), P()), check_vma=False)
```

```python
import functools

import jax
import jax.numpy as jnp
from jax import lax
from jax.experimental import pallas as pl
from jax.experimental.pallas import tpu as pltpu
from jax.sharding import PartitionSpec as P

LAGS = 4
DELAY = 1024
N = 128
COLS = LAGS * N
HALF = DELAY // 2
SPAN = DELAY + HALF
AXES = ("grp", "span")
HIGHEST = lax.Precision.HIGHEST
VMEM_LIMIT = 48 * 2**20

PAIRS = [(i, j) for i in range(LAGS) for j in range(i, LAGS)]
GRAM = {pair: index for index, pair in enumerate(PAIRS)}
CROSS = {(i, j): len(PAIRS) + LAGS * i + j for i in range(LAGS) for j in range(LAGS)}
BLOCKS = len(GRAM) + len(CROSS)
SIDE = BLOCKS // 2
CHIPS_X = 4


def exact(left, right, dims):
    return lax.dot_general(left, right, (dims, ((), ())), precision=HIGHEST, preferred_element_type=jnp.float32)


def rows_product(left, right):
    return lax.dot_general(left, right, (((0,), (0,)), ((), ())), preferred_element_type=jnp.float32)


def parts(value):
    high = value.astype(jnp.bfloat16)
    low = (value - high.astype(jnp.float32)).astype(jnp.bfloat16)
    return jnp.concatenate([high, low], 1)


def fold(value):
    return (value[:N, :N] + value[N:, :N]) + (value[:N, N:] + value[N:, N:])


def lag_products(left, right, zero_lag=False):
    first = rows_product(left, right[:, : 2 * N])
    same, back = fold(first[: 2 * N]), fold(first[2 * N :])
    ahead = None if zero_lag else fold(rows_product(left[:, : 2 * N], right[:, 2 * N :]))
    return same, back, ahead


def local_kernel(edge_ref, rec_ref, out_ref, split_ref, same_ref, back_ref, ahead_ref):
    count = rec_ref.shape[0]
    for q in range(LAGS):
        lo, hi = q * DELAY, (q + 1) * DELAY
        split_ref[lo:hi, : 2 * N] = parts(rec_ref[lo:hi, :])
        if q < LAGS - 1:
            following = rec_ref[lo + 1 : hi + 1, :]
        else:
            following = jnp.concatenate([rec_ref[lo + 1 : hi, :], jnp.zeros((1, N), jnp.float32)], 0)
        split_ref[lo:hi, 2 * N :] = parts(following)
    for q in range(LAGS):
        left = split_ref[q * DELAY : (q + 1) * DELAY, :]
        for d in range(LAGS - q):
            right = split_ref[(q + d) * DELAY : (q + d + 1) * DELAY, :]
            same, back, ahead = lag_products(left, right, d == 0)
            same_ref[LAGS * q + d] = same
            back_ref[LAGS * q + d] = back
            if d:
                ahead_ref[LAGS * q + d] = ahead
    first, last = edge_ref[0], edge_ref[1]

    def kept(q, m):
        if q < m:
            return (1 - first).astype(jnp.float32)
        if q > m:
            return (1 - last).astype(jnp.float32)
        return None

    def total(ref, d, m):
        value = None
        for q in range(LAGS - d):
            factor, term = kept(q, m), ref[LAGS * q + d]
            term = term if factor is None else term * factor
            value = term if value is None else value + term
        return value

    for i, j in PAIRS:
        d = j - i
        out_ref[GRAM[i, j]] = total(same_ref, d, i)
        out_ref[CROSS[j, i]] = total(back_ref, d, i)
        if d:
            out_ref[CROSS[i, j]] = total(ahead_ref, d, i)

    @pl.when(first + last > 0)
    def _():
        def wide(offset, steps):
            pieces = [rec_ref[offset + k * DELAY : offset + k * DELAY + 1, :] for k in range(steps)]
            pieces += [jnp.zeros((1, N), jnp.float32)] * (LAGS - steps)
            return jnp.concatenate(pieces, 1)

        start = wide(0, LAGS) * first.astype(jnp.float32)
        final = wide(DELAY - 1, LAGS) * last.astype(jnp.float32)
        after = wide(DELAY, LAGS - 1)
        blank = jnp.zeros((6, COLS), jnp.float32)
        ends = jnp.concatenate([start, final, blank], 0)
        steps = jnp.concatenate([jnp.zeros((1, COLS), jnp.float32), after, blank], 0)
        outer = ((0,), (0,))
        for i in range(LAGS):
            for j in range(LAGS):
                a, b = ends[:, i * N : (i + 1) * N], ends[:, j * N : (j + 1) * N]
                c = steps[:, j * N : (j + 1) * N]
                if j >= i:
                    out_ref[GRAM[i, j]] -= 0.5 * exact(a, b, outer)
                out_ref[CROSS[i, j]] -= exact(c, a, outer) if i >= j else exact(a, c, outer)


def carve_kernel(rec_ref, head_ref, rear_ref, sems):
    head, rear = head_ref.shape[0], rear_ref.shape[0]
    copies = [
        pltpu.make_async_copy(rec_ref.at[:head], head_ref, sems.at[0]),
        pltpu.make_async_copy(rec_ref.at[rec_ref.shape[0] - rear :], rear_ref, sems.at[1]),
    ]
    for copy in copies:
        copy.start()
    for copy in copies:
        copy.wait()


def fan_kernel(in_ref, out_ref):
    value = in_ref[0]
    for k in range(1, in_ref.shape[0]):
        value = value + in_ref[k]
    for k in range(out_ref.shape[0]):
        out_ref[k] = value


def halo_kernel(edge_ref, acc_ref, split_ref, down_ref, up_ref, keep_ref, give_ref, below, above, stage):
    below[:, : 2 * N] = parts(down_ref[:SPAN, :])
    below[:, 2 * N :] = parts(down_ref[1 : SPAN + 1, :])
    above[:, : 2 * N] = parts(up_ref[...])
    own = split_ref[0:16, : 2 * N].astype(jnp.float32)[0:1]
    own = (own[:, :N] + own[:, N:]) * (1 - edge_ref[0]).astype(jnp.float32)
    above[:, 2 * N :] = parts(jnp.concatenate([up_ref[1:SPAN, :], own], 0))

    def own_rows(start, size):
        return split_ref[start : start + size, :]

    pairs = {
        1: [(own_rows(3 * DELAY, DELAY), below[:DELAY, :])],
        2: [(own_rows(2 * DELAY, DELAY), below[:DELAY, :]), (above[HALF:, :], own_rows(DELAY, DELAY))],
        3: [
            (own_rows(DELAY, DELAY), below[:DELAY, :]),
            (above[HALF:, :], own_rows(2 * DELAY, DELAY)),
            (own_rows(2 * DELAY, HALF), below[DELAY:, :]),
            (above[:HALF, :], own_rows(DELAY + HALF, HALF)),
        ],
    }
    core = edge_ref[2]

    def put(index, value):
        stage[(index // SIDE) ^ core, index % SIDE] = value

    lastrow = lax.broadcasted_iota(jnp.int32, (16, N), 0) == 15
    entering = parts(jnp.where(lastrow, jnp.broadcast_to(down_ref[0:1, :], (16, N)), 0.0))
    count = LAGS * DELAY
    fix = fold(rows_product(entering, split_ref[count - 16 : count, : 2 * N]))
    for i in range(LAGS):
        put(GRAM[i, i], acc_ref[GRAM[i, i]])
        put(CROSS[i, i], acc_ref[CROSS[i, i]] + fix)
    for d in range(1, LAGS):
        stop = (LAGS - d) * DELAY
        same = None
        back = fold(rows_product(entering, below[DELAY - 16 : DELAY, : 2 * N])) if d == 1 else None
        ahead = fold(rows_product(split_ref[stop - 16 : stop, : 2 * N], entering))
        for left, right in pairs[d]:
            s, b, a = lag_products(left, right)
            same = s if same is None else same + s
            back = b if back is None else back + b
            ahead = ahead + a
        for i in range(LAGS - d):
            j = i + d
            put(GRAM[i, j], acc_ref[GRAM[i, j]] + same)
            put(CROSS[j, i], acc_ref[CROSS[j, i]] + back)
            put(CROSS[i, j], acc_ref[CROSS[i, j]] + ahead)
    keep_ref[...] = stage[0]
    give_ref[...] = stage[1]


def lanes(value, j):
    return jnp.broadcast_to(value[:, j : j + 1], (value.shape[0], N))


def line(value, t, n):
    return jnp.broadcast_to(value[t : t + 1, :], (n, N))


def factor(rest, inverse):
    sub = lax.broadcasted_iota(jnp.int32, (8, N), 0)
    lane = lax.broadcasted_iota(jnp.int32, (8, N), 1)
    uppers, inverses = [], []
    for k in range(N // 8):
        n = rest.shape[0] - 8
        top, top_inverse = rest[:8], inverse[:8]
        cols = [lanes(top, 8 * k + t) for t in range(8)]
        if n:
            rest, inverse = rest[8:], inverse[8:]
            below = [lanes(rest, 8 * k + t) for t in range(8)]
        pivots = jnp.zeros((8, N), jnp.float32)
        for t in range(8):
            pivot = line(cols[t], t, 8)
            recip = 1.0 / pivot
            mult = jnp.where(sub > t, cols[t] * recip, 0.0)
            if n:
                mult_below = below[t] * jnp.broadcast_to(recip[:1], (n, N))
            for u in range(t + 1, 8):
                entry = cols[u][t : t + 1, :]
                if n:
                    below[u] = below[u] - mult_below * jnp.broadcast_to(entry, (n, N))
                cols[u] = cols[u] - mult * jnp.broadcast_to(entry, (8, N))
            pivots = jnp.where(sub == t, pivot, pivots)
            if n:
                rest = rest - mult_below * line(top, t, n)
                inverse = inverse - mult_below * line(top_inverse, t, n)
            top = top - mult * line(top, t, 8)
            top_inverse = top_inverse - mult * line(top_inverse, t, 8)
        root = lax.rsqrt(pivots)
        uppers.append(jnp.where(lane >= sub + 8 * k, top * root, 0.0))
        inverses.append(top_inverse * root)
    return jnp.concatenate(uppers, 0), jnp.concatenate(inverses, 0)


def tail_kernel(scale, edge_ref, mine_ref, other_ref, tri_ref, op_ref, work, right, inv):
    core = edge_ref[2]

    def summed(index):
        a, b = mine_ref[index % SIDE], other_ref[index % SIDE]
        return jnp.where(core == index // SIDE, a, b)

    for i in range(LAGS):
        for j in range(LAGS):
            if j >= i:
                work[i, :, j * N : (j + 1) * N] = summed(GRAM[i, j]) * scale
            block = summed(CROSS[i, j])
            work[i, :, COLS + j * N : COLS + (j + 1) * N] = (block.T if i >= j else block) * scale
    rows = lax.broadcasted_iota(jnp.int32, (N, N), 0)
    eye = jnp.where(rows == lax.broadcasted_iota(jnp.int32, (N, N), 1), 1.0, 0.0).astype(jnp.float32)
    for k in range(LAGS):
        for j in range(k):
            tri_ref[k * N : (k + 1) * N, j * N : (j + 1) * N] = jnp.zeros((N, N), jnp.float32)

    def finish(k, upper, inverse):
        tri_ref[k * N : (k + 1) * N, k * N : (k + 1) * N] = upper
        solved = exact(inverse, work[k, :, (k + 1) * N :], ((1,), (0,)))
        work[k, :, (k + 1) * N :] = solved
        if k < LAGS - 1:
            tri_ref[k * N : (k + 1) * N, (k + 1) * N :] = solved[:, : (LAGS - 1 - k) * N]
        for i in range(k + 1, LAGS):
            lo = (i - k - 1) * N
            work[i, :, i * N :] = work[i, :, i * N :] - exact(solved[:, lo : lo + N], solved[:, lo:], ((0,), (0,)))

    def step(k, carry):
        upper, inverse = factor(work[k, :, pl.ds(pl.multiple_of(k * N, N), N)], eye)
        inv[k] = inverse
        for which in range(LAGS):
            pl.when(k == which)(functools.partial(finish, which, upper, inverse))
        return carry

    lax.fori_loop(0, LAGS, step, 0)
    for i in range(LAGS):
        right[i * N : (i + 1) * N, :] = work[i, :, COLS:]
    for j in range(LAGS):
        lo, hi = j * N, (j + 1) * N
        solved = exact(right[:, lo:hi], inv[j], ((1,), (1,)))
        op_ref[:, lo:hi] = solved
        if j < LAGS - 1:
            right[:, hi:] = right[:, hi:] - exact(solved, tri_ref[lo:hi, hi:], ((1,), (0,)))


def shifted(value, steps):
    count = lax.axis_size(AXES)
    leading, last = (max(0, -steps), min(count, count - steps))
    return lax.ppermute(value, AXES, [(source, source + steps) for source in range(leading, last)])


def trade(value, groups):
    if len(groups[0]) == 1:
        return value
    return lax.all_to_all(value, AXES, 0, 0, axis_index_groups=groups)


def fan(value, copies):
    return pl.pallas_call(
        fan_kernel,
        out_shape=jax.ShapeDtypeStruct((copies,) + value.shape[1:], jnp.float32),
        in_specs=[pl.BlockSpec(memory_space=pltpu.VMEM)],
        out_specs=pl.BlockSpec(memory_space=pltpu.VMEM),
        compiler_params=pltpu.CompilerParams(vmem_limit_bytes=VMEM_LIMIT),
        name="add_and_repeat",
    )(value)


def across_cores(value):
    count = lax.axis_size("grp")
    return lax.ppermute(value, "grp", [(source, source ^ 1) for source in range(count)])


def spread_sum(keep, give):
    rows, depth = lax.axis_size("grp") // 2, lax.axis_size("span") // CHIPS_X

    def device(y, core, z, x):
        return ((y * 2 + core) * depth + z) * CHIPS_X + x

    planes = [
        [device(y, core, z, x) for y in range(rows) for x in range(CHIPS_X)] for core in range(2) for z in range(depth)
    ]
    columns = [
        [device(y, core, z, x) for z in range(depth)]
        for y in range(rows)
        for core in range(2)
        for x in range(CHIPS_X)
    ]
    plane = rows * CHIPS_X
    half = keep + across_cores(give)
    shares = trade(half.reshape(plane, SIDE * N // plane, N), planes)
    shares = trade(fan(shares, depth), columns)
    mine = trade(fan(shares, plane), planes).reshape(SIDE, N, N)
    return mine, across_cores(mine)


def averaged_blocks(record, edge):
    count = record.shape[0]
    smem, vmem = pl.BlockSpec(memory_space=pltpu.SMEM), pl.BlockSpec(memory_space=pltpu.VMEM)
    anywhere = pl.BlockSpec(memory_space=pl.ANY)
    params = pltpu.CompilerParams(vmem_limit_bytes=VMEM_LIMIT)
    head, rear = pl.pallas_call(
        carve_kernel,
        out_shape=[jax.ShapeDtypeStruct((SPAN + 8, N), jnp.float32), jax.ShapeDtypeStruct((SPAN, N), jnp.float32)],
        in_specs=[anywhere],
        out_specs=[vmem, vmem],
        scratch_shapes=[pltpu.SemaphoreType.DMA((2,))],
        compiler_params=params,
        name="carve",
    )(record)
    down, up = shifted(head, -1), shifted(rear, 1)
    local, split = pl.pallas_call(
        local_kernel,
        out_shape=[
            jax.ShapeDtypeStruct((BLOCKS, N, N), jnp.float32),
            jax.ShapeDtypeStruct((count, 4 * N), jnp.bfloat16),
        ],
        in_specs=[smem, vmem],
        out_specs=[vmem, vmem],
        scratch_shapes=[pltpu.VMEM((LAGS * LAGS, N, N), jnp.float32)] * 3,
        compiler_params=params,
        cost_estimate=pl.CostEstimate(flops=4 * 10**9, bytes_accessed=8 * 2**20, transcendentals=0),
        name="local_products",
    )(edge, record)
    side = jax.ShapeDtypeStruct((SIDE, N, N), jnp.float32)
    keep, give = pl.pallas_call(
        halo_kernel,
        out_shape=[side, side],
        in_specs=[smem, vmem, vmem, vmem, vmem],
        out_specs=[vmem, vmem],
        scratch_shapes=[pltpu.VMEM((SPAN, 4 * N), jnp.bfloat16)] * 2 + [pltpu.VMEM((2, SIDE, N, N), jnp.float32)],
        compiler_params=params,
        cost_estimate=pl.CostEstimate(flops=3 * 10**9, bytes_accessed=9 * 2**20, transcendentals=0),
        name="halo_products",
    )(edge, local, split, down, up)
    return spread_sum(keep, give)


def on_device(record):
    devices = lax.axis_size(AXES)
    last_row = record.shape[0] * devices - (LAGS - 1) * DELAY - 1
    index = lax.axis_index(AXES)
    edge = jnp.stack([index == 0, index == devices - 1, lax.axis_index("grp") % 2]).astype(jnp.int32)
    mine, other = averaged_blocks(record, edge)
    smem, vmem = pl.BlockSpec(memory_space=pltpu.SMEM), pl.BlockSpec(memory_space=pltpu.VMEM)
    square = jax.ShapeDtypeStruct((COLS, COLS), jnp.float32)
    return tuple(
        pl.pallas_call(
            functools.partial(tail_kernel, 1.0 / last_row),
            out_shape=[square, square],
            in_specs=[smem, vmem, vmem],
            out_specs=[vmem, vmem],
            scratch_shapes=[
                pltpu.VMEM((LAGS, N, 2 * COLS), jnp.float32),
                pltpu.VMEM((COLS, COLS), jnp.float32),
                pltpu.VMEM((LAGS, N, N), jnp.float32),
            ],
            compiler_params=pltpu.CompilerParams(vmem_limit_bytes=VMEM_LIMIT),
            name="factor_and_solve",
        )(edge, mine, other)
    )


def solution(mesh):
    placed = (P(AXES, None),)
    return jax.shard_map(on_device, mesh=mesh, in_specs=placed, out_specs=(P(), P()), check_vma=False)
```

```python
import functools

import jax
import jax.numpy as jnp
from jax import lax
from jax.experimental import pallas as pl
from jax.experimental.pallas import tpu as pltpu
from jax.sharding import PartitionSpec as P

LAGS = 4
DELAY = 1024
N = 128
COLS = LAGS * N
HALF = DELAY // 2
SPAN = DELAY + HALF
AXES = ("grp", "span")
HIGHEST = lax.Precision.HIGHEST
VMEM_LIMIT = 48 * 2**20

PAIRS = [(i, j) for i in range(LAGS) for j in range(i, LAGS)]
GRAM = {pair: index for index, pair in enumerate(PAIRS)}
CROSS = {(i, j): len(PAIRS) + LAGS * i + j for i in range(LAGS) for j in range(LAGS)}
BLOCKS = len(GRAM) + len(CROSS)
GRAM_SIDE, CROSS_SIDE = len(GRAM) // 2, len(CROSS) // 2
CHIPS_X = 4
GROUP = 4


def exact(left, right, dims):
    return lax.dot_general(left, right, (dims, ((), ())), precision=HIGHEST, preferred_element_type=jnp.float32)


def rows_product(left, right):
    return lax.dot_general(left, right, (((0,), (0,)), ((), ())), preferred_element_type=jnp.float32)


def parts(value):
    high = value.astype(jnp.bfloat16)
    low = (value - high.astype(jnp.float32)).astype(jnp.bfloat16)
    return jnp.concatenate([high, low], 1)


def fold(value):
    return (value[:N, :N] + value[N:, :N]) + (value[:N, N:] + value[N:, N:])


def lag_products(left, right, zero_lag=False):
    first = rows_product(left, right[:, : 2 * N])
    same, back = fold(first[: 2 * N]), fold(first[2 * N :])
    ahead = None if zero_lag else fold(rows_product(left[:, : 2 * N], right[:, 2 * N :]))
    return same, back, ahead


def local_kernel(edge_ref, rec_ref, out_ref, split_ref, same_ref, back_ref, ahead_ref):
    count = rec_ref.shape[0]
    for q in range(LAGS):
        lo, hi = q * DELAY, (q + 1) * DELAY
        split_ref[lo:hi, : 2 * N] = parts(rec_ref[lo:hi, :])
        if q < LAGS - 1:
            following = rec_ref[lo + 1 : hi + 1, :]
        else:
            following = jnp.concatenate([rec_ref[lo + 1 : hi, :], jnp.zeros((1, N), jnp.float32)], 0)
        split_ref[lo:hi, 2 * N :] = parts(following)
    for q in range(LAGS):
        left = split_ref[q * DELAY : (q + 1) * DELAY, :]
        for d in range(LAGS - q):
            right = split_ref[(q + d) * DELAY : (q + d + 1) * DELAY, :]
            same, back, ahead = lag_products(left, right, d == 0)
            same_ref[LAGS * q + d] = same
            back_ref[LAGS * q + d] = back
            if d:
                ahead_ref[LAGS * q + d] = ahead
    first, last = edge_ref[0], edge_ref[1]

    def kept(q, m):
        if q < m:
            return (1 - first).astype(jnp.float32)
        if q > m:
            return (1 - last).astype(jnp.float32)
        return None

    def total(ref, d, m):
        value = None
        for q in range(LAGS - d):
            factor, term = kept(q, m), ref[LAGS * q + d]
            term = term if factor is None else term * factor
            value = term if value is None else value + term
        return value

    for i, j in PAIRS:
        d = j - i
        out_ref[GRAM[i, j]] = total(same_ref, d, i)
        out_ref[CROSS[j, i]] = total(back_ref, d, i)
        if d:
            out_ref[CROSS[i, j]] = total(ahead_ref, d, i)

    @pl.when(first + last > 0)
    def _():
        def wide(offset, steps):
            pieces = [rec_ref[offset + k * DELAY : offset + k * DELAY + 1, :] for k in range(steps)]
            pieces += [jnp.zeros((1, N), jnp.float32)] * (LAGS - steps)
            return jnp.concatenate(pieces, 1)

        start = wide(0, LAGS) * first.astype(jnp.float32)
        final = wide(DELAY - 1, LAGS) * last.astype(jnp.float32)
        after = wide(DELAY, LAGS - 1)
        blank = jnp.zeros((6, COLS), jnp.float32)
        ends = jnp.concatenate([start, final, blank], 0)
        steps = jnp.concatenate([jnp.zeros((1, COLS), jnp.float32), after, blank], 0)
        outer = ((0,), (0,))
        for i in range(LAGS):
            for j in range(LAGS):
                a, b = ends[:, i * N : (i + 1) * N], ends[:, j * N : (j + 1) * N]
                c = steps[:, j * N : (j + 1) * N]
                if j >= i:
                    out_ref[GRAM[i, j]] -= 0.5 * exact(a, b, outer)
                out_ref[CROSS[i, j]] -= exact(c, a, outer) if i >= j else exact(a, c, outer)


def carve_kernel(rec_ref, head_ref, rear_ref, sems):
    head, rear = head_ref.shape[0], rear_ref.shape[0]
    copies = [
        pltpu.make_async_copy(rec_ref.at[:head], head_ref, sems.at[0]),
        pltpu.make_async_copy(rec_ref.at[rec_ref.shape[0] - rear :], rear_ref, sems.at[1]),
    ]
    for copy in copies:
        copy.start()
    for copy in copies:
        copy.wait()


def fan_kernel(in_ref, *out_refs):
    value = in_ref[0]
    for k in range(1, in_ref.shape[0]):
        value = value + in_ref[k]
    start = 0
    for out_ref in out_refs:
        size = out_ref.shape[1]
        for k in range(out_ref.shape[0]):
            out_ref[k] = value[start : start + size]
        start += size


def halo_kernel(edge_ref, acc_ref, split_ref, down_ref, up_ref, keep_ref, give_ref, below, above, gram, cross):
    below[:, : 2 * N] = parts(down_ref[:SPAN, :])
    below[:, 2 * N :] = parts(down_ref[1 : SPAN + 1, :])
    above[:, : 2 * N] = parts(up_ref[...])
    own = split_ref[0:16, : 2 * N].astype(jnp.float32)[0:1]
    own = (own[:, :N] + own[:, N:]) * (1 - edge_ref[0]).astype(jnp.float32)
    above[:, 2 * N :] = parts(jnp.concatenate([up_ref[1:SPAN, :], own], 0))

    def own_rows(start, size):
        return split_ref[start : start + size, :]

    pairs = {
        1: [(own_rows(3 * DELAY, DELAY), below[:DELAY, :])],
        2: [(own_rows(2 * DELAY, DELAY), below[:DELAY, :]), (above[HALF:, :], own_rows(DELAY, DELAY))],
        3: [
            (own_rows(DELAY, DELAY), below[:DELAY, :]),
            (above[HALF:, :], own_rows(2 * DELAY, DELAY)),
            (own_rows(2 * DELAY, HALF), below[DELAY:, :]),
            (above[:HALF, :], own_rows(DELAY + HALF, HALF)),
        ],
    }
    core = edge_ref[2]

    def put(index, value):
        if index < len(GRAM):
            index, row = index // GRAM_SIDE, index % GRAM_SIDE * N
            gram[index ^ core, row : row + N] = value
        else:
            index -= len(GRAM)
            index, row = index // CROSS_SIDE, index % CROSS_SIDE * N
            cross[index ^ core, row : row + N] = value

    lastrow = lax.broadcasted_iota(jnp.int32, (16, N), 0) == 15
    entering = parts(jnp.where(lastrow, jnp.broadcast_to(down_ref[0:1, :], (16, N)), 0.0))
    count = LAGS * DELAY
    fix = fold(rows_product(entering, split_ref[count - 16 : count, : 2 * N]))
    for i in range(LAGS):
        put(GRAM[i, i], acc_ref[GRAM[i, i]])
        put(CROSS[i, i], acc_ref[CROSS[i, i]] + fix)
    for d in range(1, LAGS):
        stop = (LAGS - d) * DELAY
        same = None
        back = fold(rows_product(entering, below[DELAY - 16 : DELAY, : 2 * N])) if d == 1 else None
        ahead = fold(rows_product(split_ref[stop - 16 : stop, : 2 * N], entering))
        for left, right in pairs[d]:
            s, b, a = lag_products(left, right)
            same = s if same is None else same + s
            back = b if back is None else back + b
            ahead = ahead + a
        for i in range(LAGS - d):
            j = i + d
            put(GRAM[i, j], acc_ref[GRAM[i, j]] + same)
            put(CROSS[j, i], acc_ref[CROSS[j, i]] + back)
            put(CROSS[i, j], acc_ref[CROSS[i, j]] + ahead)
    members = keep_ref.shape[0]
    few, many = GRAM_SIDE * N // members, CROSS_SIDE * N // members
    for side, ref in enumerate((keep_ref, give_ref)):
        for m in range(members):
            ref[m, :few] = gram[side, m * few : (m + 1) * few]
            ref[m, few:] = cross[side, m * many : (m + 1) * many]


def lanes(value, j):
    return jnp.broadcast_to(value[:, j : j + 1], (value.shape[0], N))


def line(value, t, n):
    return jnp.broadcast_to(value[t : t + 1, :], (n, N))


def three(value):
    high = value.astype(jnp.bfloat16)
    rest = value - high.astype(jnp.float32)
    mid = rest.astype(jnp.bfloat16)
    return high, mid, (rest - mid.astype(jnp.float32)).astype(jnp.bfloat16)


def stacked(left, right, dim):
    (a, b, c), (x, y, z) = three(left), three(right)
    return lax.dot_general(
        jnp.concatenate([a, a, b, a, c, b], dim),
        jnp.concatenate([x, y, x, z, x, y], 0),
        (((dim,), (0,)), ((), ())),
        preferred_element_type=jnp.float32,
    )


def factor(matrix):
    sub = lax.broadcasted_iota(jnp.int32, (8, N), 0)
    lane = lax.broadcasted_iota(jnp.int32, (8, N), 1)
    rows = [matrix[r : r + 8] for r in range(0, N, 8)]
    uppers, inverses = [], []
    for k in range(len(rows)):
        first = 8 * k
        old, inside = lane < first + 8, (lane >= first) & (lane < first + 8)
        top = rows[k]
        grown = jnp.where(lane < first, top, 0.0) + jnp.where(lane == sub + first, 1.0, 0.0)
        cols = [lanes(top, first + t) for t in range(8)]
        others = list(range(k + 1, k - k % GROUP + GROUP))
        below = {v: [lanes(rows[v], first + t) for t in range(8)] for v in others}
        for v in others:
            rows[v] = jnp.where(inside, 0.0, rows[v])
        pivots = jnp.zeros((8, N), jnp.float32)
        for t in range(8):
            pivot = line(cols[t], t, 8)
            recip = 1.0 / pivot
            mult = jnp.where(sub > t, cols[t] * recip, 0.0)
            entries = [line(cols[u], t, 8) for u in range(t + 1, 8)]
            top_line, grown_line = line(top, t, 8), line(grown, t, 8)
            for u, entry in zip(range(t + 1, 8), entries):
                cols[u] = cols[u] - mult * entry
            pivots = jnp.where(sub == t, pivot, pivots)
            if others:
                both = jnp.where(old, grown_line, top_line)
            for v in others:
                mult_below = below[v][t] * recip
                for u, entry in zip(range(t + 1, 8), entries):
                    below[v][u] = below[v][u] - mult_below * entry
                rows[v] = rows[v] - mult_below * both
            top = top - mult * top_line
            grown = grown - mult * grown_line
        root = lax.rsqrt(pivots)
        uppers.append(jnp.where(lane >= sub + first, top * root, 0.0))
        inverses.append(grown * root)
        end = k + 1
        if end % GROUP == 0 and end < len(rows):
            upper = jnp.concatenate(uppers[-GROUP:], 0)
            columns = lax.broadcasted_iota(jnp.int32, upper.shape, 1)
            done = jnp.where(columns < 8 * end, jnp.concatenate(inverses[-GROUP:], 0), upper)
            update = stacked(upper, done, 0)
            grouped = (lane >= 8 * (end - GROUP)) & (lane < 8 * end)
            for v in range(end, len(rows)):
                rows[v] = jnp.where(grouped, 0.0, rows[v]) - update[8 * v : 8 * v + 8]
    return jnp.concatenate(uppers, 0), jnp.concatenate(inverses, 0)


def halves(mine_ref, other_ref, side, core, index):
    return jnp.where(core == index // side, mine_ref[index % side], other_ref[index % side])


def factor_kernel(scale, edge_ref, mine_ref, other_ref, tri_ref, inv_ref, work):
    for (i, j), index in GRAM.items():
        work[i, :, j * N : (j + 1) * N] = halves(mine_ref, other_ref, GRAM_SIDE, edge_ref[2], index) * scale
    zero = jnp.zeros((N, N), jnp.float32)
    for k in range(LAGS):
        for j in range(k):
            tri_ref[k * N : (k + 1) * N, j * N : (j + 1) * N] = zero
            inv_ref[j * N : (j + 1) * N, k * N : (k + 1) * N] = zero
            work[k, :, j * N : (j + 1) * N] = zero

    def finish(k, upper, inverse):
        lo, hi = k * N, (k + 1) * N
        tri_ref[lo:hi, lo:hi] = upper
        inv_ref[lo:hi, lo:hi] = inverse
        columns = [work[k, :, j * N : (j + 1) * N] for j in range(LAGS) if j != k]
        solved = stacked(inverse, jnp.concatenate(columns, 1), 1)
        if k:
            inv_ref[lo:hi, :lo] = solved[:, :lo]
        if k == LAGS - 1:
            return
        tri_ref[lo:hi, hi:] = solved[:, lo:]
        before = [solved[:, :lo]] if k else []
        done = jnp.concatenate(before + [inverse, solved[:, lo:]], 1)
        for i in range(k + 1, LAGS):
            across = jnp.concatenate([done[:, :hi], done[:, i * N :]], 1)
            update = stacked(done[:, i * N : (i + 1) * N], across, 0)
            work[i, :, :hi] -= update[:, :hi]
            work[i, :, i * N :] -= update[:, hi:]

    def step(k, carry):
        upper, inverse = factor(work[k, :, pl.ds(pl.multiple_of(k * N, N), N)])
        for which in range(LAGS):
            pl.when(k == which)(functools.partial(finish, which, upper, inverse))
        return carry

    lax.fori_loop(0, LAGS, step, 0)


def solve_kernel(scale, edge_ref, inv_ref, mine_ref, other_ref, op_ref, work):
    for (i, j), index in CROSS.items():
        block = halves(mine_ref, other_ref, CROSS_SIDE, edge_ref[2], index - len(GRAM))
        work[i * N : (i + 1) * N, j * N : (j + 1) * N] = (block.T if i >= j else block) * scale
    for lo in reversed(range(0, COLS, N)):
        hi = lo + N
        work[lo:hi, :] = exact(inv_ref[lo:hi, :hi], work[:hi, :], ((1,), (0,)))
    for lo in range(0, COLS, N):
        hi = lo + N
        op_ref[:, lo:hi] = exact(work[:, :hi], inv_ref[lo:hi, :hi], ((1,), (1,)))


def shifted(value, steps):
    count = lax.axis_size(AXES)
    leading, last = (max(0, -steps), min(count, count - steps))
    return lax.ppermute(value, AXES, [(source, source + steps) for source in range(leading, last)])


def trade(value, groups):
    if len(groups[0]) == 1:
        return value
    return lax.all_to_all(value, AXES, 0, 0, axis_index_groups=groups)


def fan(value, copies, sizes):
    return pl.pallas_call(
        fan_kernel,
        out_shape=[jax.ShapeDtypeStruct((copies, size, N), jnp.float32) for size in sizes],
        in_specs=[pl.BlockSpec(memory_space=pltpu.VMEM)],
        out_specs=[pl.BlockSpec(memory_space=pltpu.VMEM)] * len(sizes),
        compiler_params=pltpu.CompilerParams(vmem_limit_bytes=VMEM_LIMIT),
        name="add_and_repeat",
    )(value)


def across_cores(value):
    count = lax.axis_size("grp")
    return lax.ppermute(value, "grp", [(source, source ^ 1) for source in range(count)])


def spread_sum(keep, give):
    rows, depth = lax.axis_size("grp") // 2, lax.axis_size("span") // CHIPS_X

    def device(y, core, z, x):
        return ((y * 2 + core) * depth + z) * CHIPS_X + x

    planes = [
        [device(y, core, z, x) for y in range(rows) for x in range(CHIPS_X)] for core in range(2) for z in range(depth)
    ]
    columns = [
        [device(y, core, z, x) for z in range(depth)]
        for y in range(rows)
        for core in range(2)
        for x in range(CHIPS_X)
    ]
    plane = rows * CHIPS_X
    shares = trade(keep + across_cores(give), planes)
    (shares,) = fan(shares, depth, [shares.shape[1]])
    few, many = GRAM_SIDE * N // plane, CROSS_SIDE * N // plane
    gram, cross = fan(trade(shares, columns), plane, [few, many])
    gram = trade(gram, planes)
    gram, cross = lax.optimization_barrier((gram, cross))
    gram = gram.reshape(GRAM_SIDE, N, N)
    cross = trade(cross, planes).reshape(CROSS_SIDE, N, N)
    return (gram, across_cores(gram)), cross


def averaged_blocks(record, edge):
    count = record.shape[0]
    smem, vmem = pl.BlockSpec(memory_space=pltpu.SMEM), pl.BlockSpec(memory_space=pltpu.VMEM)
    params = pltpu.CompilerParams(vmem_limit_bytes=VMEM_LIMIT)
    head, rear = pl.pallas_call(
        carve_kernel,
        out_shape=[jax.ShapeDtypeStruct((SPAN + 8, N), jnp.float32), jax.ShapeDtypeStruct((SPAN, N), jnp.float32)],
        in_specs=[pl.BlockSpec(memory_space=pltpu.HBM)],
        out_specs=[vmem, vmem],
        scratch_shapes=[pltpu.SemaphoreType.DMA((2,))],
        compiler_params=pltpu.CompilerParams(vmem_limit_bytes=62 * 2**20),
        name="carve",
    )(record)
    down, up = shifted(head, -1), shifted(rear, 1)
    local, split = pl.pallas_call(
        local_kernel,
        out_shape=[
            jax.ShapeDtypeStruct((BLOCKS, N, N), jnp.float32),
            jax.ShapeDtypeStruct((count, 4 * N), jnp.bfloat16),
        ],
        in_specs=[smem, vmem],
        out_specs=[vmem, vmem],
        scratch_shapes=[pltpu.VMEM((LAGS * LAGS, N, N), jnp.float32)] * 3,
        compiler_params=params,
        cost_estimate=pl.CostEstimate(flops=4 * 10**9, bytes_accessed=8 * 2**20, transcendentals=0),
        name="local_products",
    )(edge, record)
    members = lax.axis_size("grp") // 2 * CHIPS_X
    side = jax.ShapeDtypeStruct((members, (GRAM_SIDE + CROSS_SIDE) * N // members, N), jnp.float32)
    keep, give = pl.pallas_call(
        halo_kernel,
        out_shape=[side, side],
        in_specs=[smem, vmem, vmem, vmem, vmem],
        out_specs=[vmem, vmem],
        scratch_shapes=[pltpu.VMEM((SPAN, 4 * N), jnp.bfloat16)] * 2
        + [pltpu.VMEM((2, GRAM_SIDE * N, N), jnp.float32), pltpu.VMEM((2, CROSS_SIDE * N, N), jnp.float32)],
        compiler_params=params,
        cost_estimate=pl.CostEstimate(flops=3 * 10**9, bytes_accessed=9 * 2**20, transcendentals=0),
        name="halo_products",
    )(edge, local, split, down, up)
    return spread_sum(keep, give)


def on_device(record):
    devices = lax.axis_size(AXES)
    last_row = record.shape[0] * devices - (LAGS - 1) * DELAY - 1
    index = lax.axis_index(AXES)
    edge = jnp.stack([index == 0, index == devices - 1, lax.axis_index("grp") % 2]).astype(jnp.int32)
    gram, cross = averaged_blocks(record, edge)
    smem, vmem = pl.BlockSpec(memory_space=pltpu.SMEM), pl.BlockSpec(memory_space=pltpu.VMEM)
    params = pltpu.CompilerParams(vmem_limit_bytes=VMEM_LIMIT)
    square = jax.ShapeDtypeStruct((COLS, COLS), jnp.float32)
    triangle, inverse = pl.pallas_call(
        functools.partial(factor_kernel, 1.0 / last_row),
        out_shape=[square, square],
        in_specs=[smem, vmem, vmem],
        out_specs=[vmem, vmem],
        scratch_shapes=[pltpu.VMEM((LAGS, N, COLS), jnp.float32)],
        compiler_params=params,
        cost_estimate=pl.CostEstimate(flops=20 * 10**9, bytes_accessed=4 * 2**20, transcendentals=0),
        name="factor",
    )(edge, *gram)
    cross, triangle, inverse = lax.optimization_barrier((cross, triangle, inverse))
    operator = pl.pallas_call(
        functools.partial(solve_kernel, 1.0 / last_row),
        out_shape=square,
        in_specs=[smem] + [vmem] * 3,
        out_specs=vmem,
        scratch_shapes=[pltpu.VMEM((COLS, COLS), jnp.float32)],
        compiler_params=params,
        cost_estimate=pl.CostEstimate(flops=5 * 10**9, bytes_accessed=4 * 2**20, transcendentals=0),
        name="solve",
    )(edge, inverse, cross, across_cores(cross))
    return triangle, operator


def solution(mesh):
    placed = (P(AXES, None),)
    return jax.shard_map(on_device, mesh=mesh, in_specs=placed, out_specs=(P(), P()), check_vma=False)
```

```python
import functools

import jax
import jax.numpy as jnp
from jax import lax
from jax.experimental import pallas as pl
from jax.experimental.pallas import tpu as pltpu
from jax.sharding import PartitionSpec as P

LAGS = 4
DELAY = 1024
N = 128
COLS = LAGS * N
CUT = 640
DOWN, UP = DELAY + CUT, 2 * DELAY - CUT
AXES = ("grp", "span")
HIGHEST = lax.Precision.HIGHEST
VMEM_LIMIT = 24 * 2**20

PAIRS = [(i, j) for i in range(LAGS) for j in range(i, LAGS)]
GRAM = {pair: index for index, pair in enumerate(PAIRS)}
CROSS = {(i, j): len(PAIRS) + LAGS * i + j for i in range(LAGS) for j in range(LAGS)}
BLOCKS = len(GRAM) + len(CROSS)
GRAM_SIDE, CROSS_SIDE = len(GRAM) // 2, len(CROSS) // 2
CHIPS_X = 4
GROUP = 4


def exact(left, right, dims):
    return lax.dot_general(left, right, (dims, ((), ())), precision=HIGHEST, preferred_element_type=jnp.float32)


def rows_product(left, right):
    return lax.dot_general(left, right, (((0,), (0,)), ((), ())), preferred_element_type=jnp.float32)


def parts(value):
    high = value.astype(jnp.bfloat16)
    low = (value - high.astype(jnp.float32)).astype(jnp.bfloat16)
    return jnp.concatenate([high, low], 1)


def fold(value):
    return (value[:N, :N] + value[N:, :N]) + (value[:N, N:] + value[N:, N:])


def lag_products(left, right, zero_lag=False):
    first = rows_product(left, right[:, : 2 * N])
    same, back = fold(first[: 2 * N]), fold(first[2 * N :])
    ahead = None if zero_lag else fold(rows_product(left[:, : 2 * N], right[:, 2 * N :]))
    return same, back, ahead


def local_kernel(edge_ref, rec_ref, out_ref, split_ref, same_ref, back_ref, ahead_ref):
    count = rec_ref.shape[0]
    for q in range(LAGS):
        lo, hi = q * DELAY, (q + 1) * DELAY
        split_ref[lo:hi, : 2 * N] = parts(rec_ref[lo:hi, :])
        if q < LAGS - 1:
            following = rec_ref[lo + 1 : hi + 1, :]
        else:
            following = jnp.concatenate([rec_ref[lo + 1 : hi, :], jnp.zeros((1, N), jnp.float32)], 0)
        split_ref[lo:hi, 2 * N :] = parts(following)
    for q in range(LAGS):
        left = split_ref[q * DELAY : (q + 1) * DELAY, :]
        for d in range(LAGS - q):
            right = split_ref[(q + d) * DELAY : (q + d + 1) * DELAY, :]
            same, back, ahead = lag_products(left, right, d == 0)
            same_ref[LAGS * q + d] = same
            back_ref[LAGS * q + d] = back
            if d:
                ahead_ref[LAGS * q + d] = ahead
    first, last = edge_ref[0], edge_ref[1]

    def kept(q, m):
        if q < m:
            return (1 - first).astype(jnp.float32)
        if q > m:
            return (1 - last).astype(jnp.float32)
        return None

    def total(ref, d, m):
        value = None
        for q in range(LAGS - d):
            factor, term = kept(q, m), ref[LAGS * q + d]
            term = term if factor is None else term * factor
            value = term if value is None else value + term
        return value

    for i, j in PAIRS:
        d = j - i
        out_ref[GRAM[i, j]] = total(same_ref, d, i)
        out_ref[CROSS[j, i]] = total(back_ref, d, i)
        if d:
            out_ref[CROSS[i, j]] = total(ahead_ref, d, i)

    @pl.when(first + last > 0)
    def _():
        def wide(offset, steps):
            pieces = [rec_ref[offset + k * DELAY : offset + k * DELAY + 1, :] for k in range(steps)]
            pieces += [jnp.zeros((1, N), jnp.float32)] * (LAGS - steps)
            return jnp.concatenate(pieces, 1)

        start = wide(0, LAGS) * first.astype(jnp.float32)
        final = wide(DELAY - 1, LAGS) * last.astype(jnp.float32)
        after = wide(DELAY, LAGS - 1)
        blank = jnp.zeros((6, COLS), jnp.float32)
        ends = jnp.concatenate([start, final, blank], 0)
        steps = jnp.concatenate([jnp.zeros((1, COLS), jnp.float32), after, blank], 0)
        outer = ((0,), (0,))
        for i in range(LAGS):
            for j in range(LAGS):
                a, b = ends[:, i * N : (i + 1) * N], ends[:, j * N : (j + 1) * N]
                c = steps[:, j * N : (j + 1) * N]
                if j >= i:
                    out_ref[GRAM[i, j]] -= 0.5 * exact(a, b, outer)
                out_ref[CROSS[i, j]] -= exact(c, a, outer) if i >= j else exact(a, c, outer)


def carve_kernel(rec_ref, head_ref, rear_ref, sems):
    head, rear = head_ref.shape[0], rear_ref.shape[0]
    copies = [
        pltpu.make_async_copy(rec_ref.at[:head], head_ref, sems.at[0]),
        pltpu.make_async_copy(rec_ref.at[rec_ref.shape[0] - rear :], rear_ref, sems.at[1]),
    ]
    for copy in copies:
        copy.start()
    for copy in copies:
        copy.wait()


def fan_kernel(in_ref, out_ref):
    value = in_ref[0]
    for k in range(1, in_ref.shape[0]):
        value = value + in_ref[k]
    for k in range(out_ref.shape[0]):
        out_ref[k] = value


def halo_kernel(edge_ref, acc_ref, split_ref, down_ref, up_ref, keep_ref, give_ref, below, above, gram, cross):
    below[:, : 2 * N] = parts(down_ref[:DOWN, :])
    below[:, 2 * N :] = parts(down_ref[1 : DOWN + 1, :])
    above[:, : 2 * N] = parts(up_ref[...])
    own = split_ref[0:16, : 2 * N].astype(jnp.float32)[0:1]
    own = (own[:, :N] + own[:, N:]) * (1 - edge_ref[0]).astype(jnp.float32)
    above[:, 2 * N :] = parts(jnp.concatenate([up_ref[1:UP, :], own], 0))

    def own_rows(start, size):
        return split_ref[start : start + size, :]

    pairs = {
        1: [(own_rows(3 * DELAY, DELAY), below[:DELAY, :])],
        2: [(own_rows(2 * DELAY, DELAY), below[:DELAY, :]), (above[DELAY - CUT :, :], own_rows(DELAY, DELAY))],
        3: [
            (own_rows(DELAY, DELAY), below[:DELAY, :]),
            (above[DELAY - CUT :, :], own_rows(2 * DELAY, DELAY)),
            (own_rows(2 * DELAY, CUT), below[DELAY:, :]),
            (above[: DELAY - CUT, :], own_rows(DELAY + CUT, DELAY - CUT)),
        ],
    }
    core = edge_ref[2]

    def put(index, value):
        if index < len(GRAM):
            index, row = index // GRAM_SIDE, index % GRAM_SIDE * N
            gram[index ^ core, row : row + N] = value
        else:
            index -= len(GRAM)
            index, row = index // CROSS_SIDE, index % CROSS_SIDE * N
            cross[index ^ core, row : row + N] = value

    lastrow = lax.broadcasted_iota(jnp.int32, (16, N), 0) == 15
    entering = parts(jnp.where(lastrow, jnp.broadcast_to(down_ref[0:1, :], (16, N)), 0.0))
    count = LAGS * DELAY
    fix = fold(rows_product(entering, split_ref[count - 16 : count, : 2 * N]))
    for i in range(LAGS):
        put(GRAM[i, i], acc_ref[GRAM[i, i]])
        put(CROSS[i, i], acc_ref[CROSS[i, i]] + fix)
    for d in range(1, LAGS):
        stop = (LAGS - d) * DELAY
        same = None
        back = fold(rows_product(entering, below[DELAY - 16 : DELAY, : 2 * N])) if d == 1 else None
        ahead = fold(rows_product(split_ref[stop - 16 : stop, : 2 * N], entering))
        for left, right in pairs[d]:
            s, b, a = lag_products(left, right)
            same = s if same is None else same + s
            back = b if back is None else back + b
            ahead = ahead + a
        for i in range(LAGS - d):
            j = i + d
            put(GRAM[i, j], acc_ref[GRAM[i, j]] + same)
            put(CROSS[j, i], acc_ref[CROSS[j, i]] + back)
            put(CROSS[i, j], acc_ref[CROSS[i, j]] + ahead)
    members = keep_ref.shape[0]
    few, many = GRAM_SIDE * N // members, CROSS_SIDE * N // members
    for side, ref in enumerate((keep_ref, give_ref)):
        for m in range(members):
            ref[m, :few] = gram[side, m * few : (m + 1) * few]
            ref[m, few:] = cross[side, m * many : (m + 1) * many]


def lanes(value, j):
    return jnp.broadcast_to(value[:, j : j + 1], (value.shape[0], N))


def line(value, t, n):
    return jnp.broadcast_to(value[t : t + 1, :], (n, N))


def three(value):
    high = value.astype(jnp.bfloat16)
    rest = value - high.astype(jnp.float32)
    mid = rest.astype(jnp.bfloat16)
    return high, mid, (rest - mid.astype(jnp.float32)).astype(jnp.bfloat16)


def stacked(left, right, left_dim, right_dim):
    (a, b, c), (x, y, z) = three(left), three(right)
    return lax.dot_general(
        jnp.concatenate([a, a, b, a, c, b], left_dim),
        jnp.concatenate([x, y, x, z, x, y], right_dim),
        (((left_dim,), (right_dim,)), ((), ())),
        preferred_element_type=jnp.float32,
    )


def factor(matrix):
    sub = lax.broadcasted_iota(jnp.int32, (8, N), 0)
    lane = lax.broadcasted_iota(jnp.int32, (8, N), 1)
    rows = [matrix[r : r + 8] for r in range(0, N, 8)]
    uppers, inverses = [], []
    for k in range(len(rows)):
        first = 8 * k
        old, inside = lane < first + 8, (lane >= first) & (lane < first + 8)
        top = rows[k]
        grown = jnp.where(lane < first, top, 0.0) + jnp.where(lane == sub + first, 1.0, 0.0)
        cols = [lanes(top, first + t) for t in range(8)]
        others = list(range(k + 1, k - k % GROUP + GROUP))
        below = {v: [lanes(rows[v], first + t) for t in range(8)] for v in others}
        for v in others:
            rows[v] = jnp.where(inside, 0.0, rows[v])
        pivots = jnp.zeros((8, N), jnp.float32)
        for t in range(8):
            pivot = line(cols[t], t, 8)
            recip = 1.0 / pivot
            mult = jnp.where(sub > t, cols[t] * recip, 0.0)
            entries = [line(cols[u], t, 8) for u in range(t + 1, 8)]
            top_line, grown_line = line(top, t, 8), line(grown, t, 8)
            for u, entry in zip(range(t + 1, 8), entries):
                cols[u] = cols[u] - mult * entry
            pivots = jnp.where(sub == t, pivot, pivots)
            if others:
                both = jnp.where(old, grown_line, top_line)
            for v in others:
                mult_below = below[v][t] * recip
                for u, entry in zip(range(t + 1, 8), entries):
                    below[v][u] = below[v][u] - mult_below * entry
                rows[v] = rows[v] - mult_below * both
            top = top - mult * top_line
            grown = grown - mult * grown_line
        root = lax.rsqrt(pivots)
        uppers.append(jnp.where(lane >= sub + first, top * root, 0.0))
        inverses.append(grown * root)
        end = k + 1
        if end % GROUP == 0 and end < len(rows):
            upper = jnp.concatenate(uppers[-GROUP:], 0)
            columns = lax.broadcasted_iota(jnp.int32, upper.shape, 1)
            done = jnp.where(columns < 8 * end, jnp.concatenate(inverses[-GROUP:], 0), upper)
            update = stacked(upper, done, 0, 0)
            grouped = (lane >= 8 * (end - GROUP)) & (lane < 8 * end)
            for v in range(end, len(rows)):
                rows[v] = jnp.where(grouped, 0.0, rows[v]) - update[8 * v : 8 * v + 8]
    return jnp.concatenate(uppers, 0), jnp.concatenate(inverses, 0)


def tail_kernel(scale, edge_ref, mine_ref, other_ref, tri_ref, op_ref, gram, cross, work, inv, left):
    core = edge_ref[2]
    few = gram.shape[1] // mine_ref.shape[0]
    many = cross.shape[1] // mine_ref.shape[0]
    for side, ref in ((core, mine_ref), (1 - core, other_ref)):
        for m in range(ref.shape[0]):
            gram[side, m * few : (m + 1) * few] = ref[m, :few] * scale
            cross[side, m * many : (m + 1) * many] = ref[m, few:] * scale
    factor_rows(gram, tri_ref, inv, work)
    solve_rows(cross, inv, op_ref, left)


def factor_rows(gram, tri_ref, inv_ref, work):
    for (i, j), index in GRAM.items():
        row = index % GRAM_SIDE * N
        work[i, :, j * N : (j + 1) * N] = gram[index // GRAM_SIDE, row : row + N]
    zero = jnp.zeros((N, N), jnp.float32)
    for k in range(LAGS):
        for j in range(k):
            tri_ref[k * N : (k + 1) * N, j * N : (j + 1) * N] = zero
            inv_ref[j * N : (j + 1) * N, k * N : (k + 1) * N] = zero
            work[k, :, j * N : (j + 1) * N] = zero

    def finish(k, upper, inverse):
        lo, hi = k * N, (k + 1) * N
        tri_ref[lo:hi, lo:hi] = upper
        inv_ref[lo:hi, lo:hi] = inverse
        columns = [work[k, :, j * N : (j + 1) * N] for j in range(LAGS) if j != k]
        solved = stacked(inverse, jnp.concatenate(columns, 1), 1, 0)
        if k:
            inv_ref[lo:hi, :lo] = solved[:, :lo]
        if k == LAGS - 1:
            return
        tri_ref[lo:hi, hi:] = solved[:, lo:]
        before = [solved[:, :lo]] if k else []
        done = jnp.concatenate(before + [inverse, solved[:, lo:]], 1)
        for i in range(k + 1, LAGS):
            across = jnp.concatenate([done[:, :hi], done[:, i * N :]], 1)
            update = stacked(done[:, i * N : (i + 1) * N], across, 0, 0)
            work[i, :, :hi] -= update[:, :hi]
            work[i, :, i * N :] -= update[:, hi:]

    def step(k, carry):
        upper, inverse = factor(work[k, :, pl.ds(pl.multiple_of(k * N, N), N)])
        for which in range(LAGS):
            pl.when(k == which)(functools.partial(finish, which, upper, inverse))
        return carry

    lax.fori_loop(0, LAGS, step, 0)


def solve_rows(cross, inv_ref, op_ref, work):
    for (i, j), index in CROSS.items():
        index -= len(GRAM)
        row = index % CROSS_SIDE * N
        block = cross[index // CROSS_SIDE, row : row + N]
        work[i * N : (i + 1) * N, j * N : (j + 1) * N] = block.T if i >= j else block
    for lo in reversed(range(0, COLS, N)):
        hi = lo + N
        work[lo:hi, :] = stacked(inv_ref[lo:hi, :hi], work[:hi, :], 1, 0)
    for lo in range(0, COLS, N):
        hi = lo + N
        op_ref[:, lo:hi] = stacked(work[:, :hi], inv_ref[lo:hi, :hi], 1, 1)


def shifted(value, steps):
    count = lax.axis_size(AXES)
    leading, last = (max(0, -steps), min(count, count - steps))
    return lax.ppermute(value, AXES, [(source, source + steps) for source in range(leading, last)])


def trade(value, groups):
    if len(groups[0]) == 1:
        return value
    return lax.all_to_all(value, AXES, 0, 0, axis_index_groups=groups)


def fan(value, copies):
    return pl.pallas_call(
        fan_kernel,
        out_shape=jax.ShapeDtypeStruct((copies,) + value.shape[1:], jnp.float32),
        in_specs=[pl.BlockSpec(memory_space=pltpu.VMEM)],
        out_specs=pl.BlockSpec(memory_space=pltpu.VMEM),
        compiler_params=pltpu.CompilerParams(vmem_limit_bytes=VMEM_LIMIT),
        name="add_and_repeat",
    )(value)


def across_cores(value):
    count = lax.axis_size("grp")
    return lax.ppermute(value, "grp", [(source, source ^ 1) for source in range(count)])


def spread_sum(keep, give):
    rows, depth = lax.axis_size("grp") // 2, lax.axis_size("span") // CHIPS_X

    def device(y, core, z, x):
        return ((y * 2 + core) * depth + z) * CHIPS_X + x

    planes = [
        [device(y, core, z, x) for y in range(rows) for x in range(CHIPS_X)] for core in range(2) for z in range(depth)
    ]
    columns = [
        [device(y, core, z, x) for z in range(depth)]
        for y in range(rows)
        for core in range(2)
        for x in range(CHIPS_X)
    ]
    plane = rows * CHIPS_X
    shares = trade(keep + across_cores(give), planes)
    shares = fan(shares, depth)
    mine = trade(fan(trade(shares, columns), plane), planes)
    return mine, across_cores(mine)


def averaged_blocks(record, edge):
    count = record.shape[0]
    smem, vmem = pl.BlockSpec(memory_space=pltpu.SMEM), pl.BlockSpec(memory_space=pltpu.VMEM)
    params = pltpu.CompilerParams(vmem_limit_bytes=VMEM_LIMIT)
    head, rear = pl.pallas_call(
        carve_kernel,
        out_shape=[jax.ShapeDtypeStruct((DOWN + 8, N), jnp.float32), jax.ShapeDtypeStruct((UP, N), jnp.float32)],
        in_specs=[pl.BlockSpec(memory_space=pltpu.HBM)],
        out_specs=[vmem, vmem],
        scratch_shapes=[pltpu.SemaphoreType.DMA((2,))],
        compiler_params=pltpu.CompilerParams(vmem_limit_bytes=62 * 2**20),
        name="carve",
    )(record)
    down, up = shifted(head, -1), shifted(rear, 1)
    local, split = pl.pallas_call(
        local_kernel,
        out_shape=[
            jax.ShapeDtypeStruct((BLOCKS, N, N), jnp.float32),
            jax.ShapeDtypeStruct((count, 4 * N), jnp.bfloat16),
        ],
        in_specs=[smem, vmem],
        out_specs=[vmem, vmem],
        scratch_shapes=[pltpu.VMEM((LAGS * LAGS, N, N), jnp.float32)] * 3,
        compiler_params=params,
        cost_estimate=pl.CostEstimate(flops=4 * 10**9, bytes_accessed=8 * 2**20, transcendentals=0),
        name="local_products",
    )(edge, record)
    members = lax.axis_size("grp") // 2 * CHIPS_X
    side = jax.ShapeDtypeStruct((members, (GRAM_SIDE + CROSS_SIDE) * N // members, N), jnp.float32)
    keep, give = pl.pallas_call(
        halo_kernel,
        out_shape=[side, side],
        in_specs=[smem, vmem, vmem, vmem, vmem],
        out_specs=[vmem, vmem],
        scratch_shapes=[pltpu.VMEM((DOWN, 4 * N), jnp.bfloat16), pltpu.VMEM((UP, 4 * N), jnp.bfloat16)]
        + [pltpu.VMEM((2, GRAM_SIDE * N, N), jnp.float32), pltpu.VMEM((2, CROSS_SIDE * N, N), jnp.float32)],
        compiler_params=params,
        cost_estimate=pl.CostEstimate(flops=3 * 10**9, bytes_accessed=9 * 2**20, transcendentals=0),
        name="halo_products",
    )(edge, local, split, down, up)
    return spread_sum(keep, give)


def on_device(record):
    devices = lax.axis_size(AXES)
    last_row = record.shape[0] * devices - (LAGS - 1) * DELAY - 1
    index = lax.axis_index(AXES)
    edge = jnp.stack([index == 0, index == devices - 1, lax.axis_index("grp") % 2]).astype(jnp.int32)
    mine, other = averaged_blocks(record, edge)
    smem, vmem = pl.BlockSpec(memory_space=pltpu.SMEM), pl.BlockSpec(memory_space=pltpu.VMEM)
    square = jax.ShapeDtypeStruct((COLS, COLS), jnp.float32)
    return tuple(
        pl.pallas_call(
            functools.partial(tail_kernel, 1.0 / last_row),
            out_shape=[square, square],
            in_specs=[smem, vmem, vmem],
            out_specs=[vmem, vmem],
            scratch_shapes=[
                pltpu.VMEM((2, GRAM_SIDE * N, N), jnp.float32),
                pltpu.VMEM((2, CROSS_SIDE * N, N), jnp.float32),
                pltpu.VMEM((LAGS, N, COLS), jnp.float32),
                pltpu.VMEM((COLS, COLS), jnp.float32),
                pltpu.VMEM((COLS, COLS), jnp.float32),
            ],
            compiler_params=pltpu.CompilerParams(vmem_limit_bytes=VMEM_LIMIT),
            name="factor_and_solve",
        )(edge, mine, other)
    )


def solution(mesh):
    placed = (P(AXES, None),)
    return jax.shard_map(on_device, mesh=mesh, in_specs=placed, out_specs=(P(), P()), check_vma=False)
```

```python
import functools

import jax
import jax.numpy as jnp
from jax import lax
from jax.experimental import pallas as pl
from jax.experimental.pallas import tpu as pltpu
from jax.sharding import PartitionSpec as P

LAGS = 4
DELAY = 1024
N = 128
COLS = LAGS * N
CUT = 640
DOWN, UP = DELAY + CUT, 2 * DELAY - CUT
AXES = ("grp", "span")
HIGHEST = lax.Precision.HIGHEST
VMEM_LIMIT = 24 * 2**20

PAIRS = [(i, j) for i in range(LAGS) for j in range(i, LAGS)]
GRAM = {pair: index for index, pair in enumerate(PAIRS)}
CROSS = {(i, j): len(PAIRS) + LAGS * i + j for i in range(LAGS) for j in range(LAGS)}
BLOCKS = len(GRAM) + len(CROSS)
GRAM_SIDE, CROSS_SIDE = len(GRAM) // 2, len(CROSS) // 2
CHIPS_X = 4
CARVE = 2
GROUP = 4


def exact(left, right, dims):
    return lax.dot_general(left, right, (dims, ((), ())), precision=HIGHEST, preferred_element_type=jnp.float32)


def rows_product(left, right):
    return lax.dot_general(left, right, (((0,), (0,)), ((), ())), preferred_element_type=jnp.float32)


def parts(value):
    high = value.astype(jnp.bfloat16)
    low = (value - high.astype(jnp.float32)).astype(jnp.bfloat16)
    return jnp.concatenate([high, low], 1)


def fold(value):
    return (value[:N, :N] + value[N:, :N]) + (value[:N, N:] + value[N:, N:])


def lag_products(left, right, zero_lag=False):
    first = rows_product(left, right[:, : 2 * N])
    same, back = fold(first[: 2 * N]), fold(first[2 * N :])
    ahead = None if zero_lag else fold(rows_product(left[:, : 2 * N], right[:, 2 * N :]))
    return same, back, ahead


def local_kernel(edge_ref, rec_ref, out_ref, split_ref, same_ref, back_ref, ahead_ref):
    count = rec_ref.shape[0]
    for q in range(LAGS):
        lo, hi = q * DELAY, (q + 1) * DELAY
        split_ref[lo:hi, : 2 * N] = parts(rec_ref[lo:hi, :])
        if q < LAGS - 1:
            following = rec_ref[lo + 1 : hi + 1, :]
        else:
            following = jnp.concatenate([rec_ref[lo + 1 : hi, :], jnp.zeros((1, N), jnp.float32)], 0)
        split_ref[lo:hi, 2 * N :] = parts(following)
    for q in range(LAGS):
        left = split_ref[q * DELAY : (q + 1) * DELAY, :]
        for d in range(LAGS - q):
            right = split_ref[(q + d) * DELAY : (q + d + 1) * DELAY, :]
            same, back, ahead = lag_products(left, right, d == 0)
            same_ref[LAGS * q + d] = same
            back_ref[LAGS * q + d] = back
            if d:
                ahead_ref[LAGS * q + d] = ahead
    first, last = edge_ref[0], edge_ref[1]

    def kept(q, m):
        if q < m:
            return (1 - first).astype(jnp.float32)
        if q > m:
            return (1 - last).astype(jnp.float32)
        return None

    def total(ref, d, m):
        value = None
        for q in range(LAGS - d):
            factor, term = kept(q, m), ref[LAGS * q + d]
            term = term if factor is None else term * factor
            value = term if value is None else value + term
        return value

    for i, j in PAIRS:
        d = j - i
        out_ref[GRAM[i, j]] = total(same_ref, d, i)
        out_ref[CROSS[j, i]] = total(back_ref, d, i)
        if d:
            out_ref[CROSS[i, j]] = total(ahead_ref, d, i)

    @pl.when(first + last > 0)
    def _():
        def wide(offset, steps):
            pieces = [rec_ref[offset + k * DELAY : offset + k * DELAY + 1, :] for k in range(steps)]
            pieces += [jnp.zeros((1, N), jnp.float32)] * (LAGS - steps)
            return jnp.concatenate(pieces, 1)

        start = wide(0, LAGS) * first.astype(jnp.float32)
        final = wide(DELAY - 1, LAGS) * last.astype(jnp.float32)
        after = wide(DELAY, LAGS - 1)
        blank = jnp.zeros((6, COLS), jnp.float32)
        ends = jnp.concatenate([start, final, blank], 0)
        steps = jnp.concatenate([jnp.zeros((1, COLS), jnp.float32), after, blank], 0)
        outer = ((0,), (0,))
        for i in range(LAGS):
            for j in range(LAGS):
                a, b = ends[:, i * N : (i + 1) * N], ends[:, j * N : (j + 1) * N]
                c = steps[:, j * N : (j + 1) * N]
                if j >= i:
                    out_ref[GRAM[i, j]] -= 0.5 * exact(a, b, outer)
                out_ref[CROSS[i, j]] -= exact(c, a, outer) if i >= j else exact(a, c, outer)


def carve_kernel(rec_ref, head_ref, rear_ref, held, in_sems, out_sems):
    count, parts_of = rec_ref.shape[0], CARVE
    pieces = []
    for ref, start in ((head_ref, 0), (rear_ref, count - rear_ref.shape[0])):
        size = ref.shape[0] // parts_of
        pieces += [(ref, start, p * size, size) for p in range(parts_of)]
    arrivals, departures, place = [], [], 0
    for n, (ref, start, offset, size) in enumerate(pieces):
        slot = held.at[place : place + size]
        arrivals.append(pltpu.make_async_copy(rec_ref.at[start + offset : start + offset + size], slot, in_sems.at[n]))
        departures.append(pltpu.make_async_copy(slot, ref.at[offset : offset + size], out_sems.at[n]))
        place += size
    for copy in arrivals:
        copy.start()
    for arrival, departure in zip(arrivals, departures):
        arrival.wait()
        departure.start()
    for copy in departures:
        copy.wait()


def fan_kernel(in_ref, out_ref):
    value = in_ref[0]
    for k in range(1, in_ref.shape[0]):
        value = value + in_ref[k]
    for k in range(out_ref.shape[0]):
        out_ref[k] = value


def halo_kernel(edge_ref, acc_ref, split_ref, down_ref, up_ref, keep_ref, give_ref, below, above, gram, cross):
    below[:, : 2 * N] = parts(down_ref[:DOWN, :])
    below[:, 2 * N :] = parts(down_ref[1 : DOWN + 1, :])
    above[:, : 2 * N] = parts(up_ref[...])
    own = split_ref[0:16, : 2 * N].astype(jnp.float32)[0:1]
    own = (own[:, :N] + own[:, N:]) * (1 - edge_ref[0]).astype(jnp.float32)
    above[:, 2 * N :] = parts(jnp.concatenate([up_ref[1:UP, :], own], 0))

    def own_rows(start, size):
        return split_ref[start : start + size, :]

    pairs = {
        1: [(own_rows(3 * DELAY, DELAY), below[:DELAY, :])],
        2: [(own_rows(2 * DELAY, DELAY), below[:DELAY, :]), (above[DELAY - CUT :, :], own_rows(DELAY, DELAY))],
        3: [
            (own_rows(DELAY, DELAY), below[:DELAY, :]),
            (above[DELAY - CUT :, :], own_rows(2 * DELAY, DELAY)),
            (own_rows(2 * DELAY, CUT), below[DELAY:, :]),
            (above[: DELAY - CUT, :], own_rows(DELAY + CUT, DELAY - CUT)),
        ],
    }
    core = edge_ref[2]

    def put(index, value):
        if index < len(GRAM):
            index, row = index // GRAM_SIDE, index % GRAM_SIDE * N
            gram[index ^ core, row : row + N] = value
        else:
            index -= len(GRAM)
            index, row = index // CROSS_SIDE, index % CROSS_SIDE * N
            cross[index ^ core, row : row + N] = value

    lastrow = lax.broadcasted_iota(jnp.int32, (16, N), 0) == 15
    entering = parts(jnp.where(lastrow, jnp.broadcast_to(down_ref[0:1, :], (16, N)), 0.0))
    count = LAGS * DELAY
    fix = fold(rows_product(entering, split_ref[count - 16 : count, : 2 * N]))
    for i in range(LAGS):
        put(GRAM[i, i], acc_ref[GRAM[i, i]])
        put(CROSS[i, i], acc_ref[CROSS[i, i]] + fix)
    for d in range(1, LAGS):
        stop = (LAGS - d) * DELAY
        same = None
        back = fold(rows_product(entering, below[DELAY - 16 : DELAY, : 2 * N])) if d == 1 else None
        ahead = fold(rows_product(split_ref[stop - 16 : stop, : 2 * N], entering))
        for left, right in pairs[d]:
            s, b, a = lag_products(left, right)
            same = s if same is None else same + s
            back = b if back is None else back + b
            ahead = ahead + a
        for i in range(LAGS - d):
            j = i + d
            put(GRAM[i, j], acc_ref[GRAM[i, j]] + same)
            put(CROSS[j, i], acc_ref[CROSS[j, i]] + back)
            put(CROSS[i, j], acc_ref[CROSS[i, j]] + ahead)
    members = keep_ref.shape[0]
    few, many = GRAM_SIDE * N // members, CROSS_SIDE * N // members
    for side, ref in enumerate((keep_ref, give_ref)):
        for m in range(members):
            ref[m, :few] = gram[side, m * few : (m + 1) * few]
            ref[m, few:] = cross[side, m * many : (m + 1) * many]


def lanes(value, j):
    return jnp.broadcast_to(value[:, j : j + 1], (value.shape[0], N))


def line(value, t, n):
    return jnp.broadcast_to(value[t : t + 1, :], (n, N))


def three(value):
    high = value.astype(jnp.bfloat16)
    rest = value - high.astype(jnp.float32)
    mid = rest.astype(jnp.bfloat16)
    return high, mid, (rest - mid.astype(jnp.float32)).astype(jnp.bfloat16)


def stacked(left, right, left_dim, right_dim):
    (a, b, c), (x, y, z) = three(left), three(right)
    return lax.dot_general(
        jnp.concatenate([a, a, b, a, c, b], left_dim),
        jnp.concatenate([x, y, x, z, x, y], right_dim),
        (((left_dim,), (right_dim,)), ((), ())),
        preferred_element_type=jnp.float32,
    )


def factor(matrix, between):
    sub = lax.broadcasted_iota(jnp.int32, (8, N), 0)
    lane = lax.broadcasted_iota(jnp.int32, (8, N), 1)
    rows = [matrix[r : r + 8] for r in range(0, N, 8)]
    uppers, inverses = [], []
    for k in range(len(rows)):
        first = 8 * k
        old, inside = lane < first + 8, (lane >= first) & (lane < first + 8)
        top = rows[k]
        grown = jnp.where(lane < first, top, 0.0) + jnp.where(lane == sub + first, 1.0, 0.0)
        cols = [lanes(top, first + t) for t in range(8)]
        others = list(range(k + 1, k - k % GROUP + GROUP))
        below = {v: [lanes(rows[v], first + t) for t in range(8)] for v in others}
        for v in others:
            rows[v] = jnp.where(inside, 0.0, rows[v])
        pivots = jnp.zeros((8, N), jnp.float32)
        for t in range(8):
            pivot = line(cols[t], t, 8)
            recip = 1.0 / pivot
            mult = jnp.where(sub > t, cols[t] * recip, 0.0)
            entries = [line(cols[u], t, 8) for u in range(t + 1, 8)]
            top_line, grown_line = line(top, t, 8), line(grown, t, 8)
            for u, entry in zip(range(t + 1, 8), entries):
                cols[u] = cols[u] - mult * entry
            pivots = jnp.where(sub == t, pivot, pivots)
            if others:
                both = jnp.where(old, grown_line, top_line)
            for v in others:
                mult_below = below[v][t] * recip
                for u, entry in zip(range(t + 1, 8), entries):
                    below[v][u] = below[v][u] - mult_below * entry
                rows[v] = rows[v] - mult_below * both
            top = top - mult * top_line
            grown = grown - mult * grown_line
        root = lax.rsqrt(pivots)
        uppers.append(jnp.where(lane >= sub + first, top * root, 0.0))
        inverses.append(grown * root)
        between()
        end = k + 1
        if end % GROUP == 0 and end < len(rows):
            upper = jnp.concatenate(uppers[-GROUP:], 0)
            columns = lax.broadcasted_iota(jnp.int32, upper.shape, 1)
            done = jnp.where(columns < 8 * end, jnp.concatenate(inverses[-GROUP:], 0), upper)
            update = stacked(upper, done, 0, 0)
            grouped = (lane >= 8 * (end - GROUP)) & (lane < 8 * end)
            for v in range(end, len(rows)):
                rows[v] = jnp.where(grouped, 0.0, rows[v]) - update[8 * v : 8 * v + 8]
    return jnp.concatenate(uppers, 0), jnp.concatenate(inverses, 0)


def tail_kernel(scale, edge_ref, mine_ref, other_ref, tri_ref, op_ref, gram, cross, work, inv, left):
    core = edge_ref[2]
    few = gram.shape[1] // mine_ref.shape[0]
    many = cross.shape[1] // mine_ref.shape[0]
    for side, ref in ((core, mine_ref), (1 - core, other_ref)):
        for m in range(ref.shape[0]):
            gram[side, m * few : (m + 1) * few] = ref[m, :few] * scale
            cross[side, m * many : (m + 1) * many] = ref[m, few:] * scale
    factor_and_solve(gram, cross, tri_ref, op_ref, inv, work, left)


def factor_and_solve(gram, cross, tri_ref, op_ref, inv_ref, work, left):
    def block(k):
        return slice(k * N, (k + 1) * N)

    zero = jnp.zeros((N, N), jnp.float32)
    for k in range(LAGS):
        for j in range(k):
            tri_ref[block(k), block(j)] = zero
            inv_ref[block(j), block(k)] = zero
            work[block(k), block(j)] = zero
    for (i, j), index in GRAM.items():
        row = index % GRAM_SIDE * N
        work[block(i), block(j)] = gram[index // GRAM_SIDE, row : row + N]
    waiting = []

    def between():
        if waiting:
            waiting.pop(0)()

    def fetch(i, j):
        index = CROSS[i, j] - len(GRAM)
        row = index % CROSS_SIDE * N
        value = cross[index // CROSS_SIDE, row : row + N]
        left[block(i), block(j)] = value.T if i >= j else value

    def solve_side(k, inverse, target, source, columns):
        target[block(k), columns] = stacked(inverse, source[block(k), columns], 1, 0)

    def update(k, i, target, source, columns):
        target[block(i), columns] -= stacked(tri_ref[block(k), block(i)], source[block(k), columns], 0, 0)

    def project(rows, j):
        known = slice(0, (j + 1) * N)
        op_ref[rows, block(j)] = stacked(left[rows, known], inv_ref[block(j), known], 1, 1)

    def later(function, *args):
        waiting.append(functools.partial(function, *args))

    for i in range(LAGS):
        for j in range(LAGS):
            later(fetch, i, j)
    everything = slice(0, COLS)
    for k in range(LAGS):
        upper, inverse = factor(work[block(k), block(k)], between)
        while waiting:
            between()
        tri_ref[block(k), block(k)] = upper
        inv_ref[block(k), block(k)] = inverse
        if k + 1 < LAGS:
            solve_side(k, inverse, tri_ref, work, block(k + 1))
            update(k, k + 1, work, tri_ref, block(k + 1))
        if k + 2 < LAGS:
            later(solve_side, k, inverse, tri_ref, work, slice((k + 2) * N, COLS))
        if k:
            later(solve_side, k, inverse, inv_ref, work, slice(0, k * N))
        later(solve_side, k, inverse, left, left, everything)
        for i in range(k + 1, LAGS):
            start = max(i, k + 2) * N
            if start < COLS:
                later(update, k, i, work, tri_ref, slice(start, COLS))
            later(update, k, i, work, inv_ref, slice(0, (k + 1) * N))
            later(update, k, i, left, left, everything)
        if k == LAGS - 2:
            for j in range(LAGS - 1):
                later(project, slice(0, (LAGS - 1) * N), j)
    while waiting:
        between()
    for j in range(LAGS - 1):
        project(block(LAGS - 1), j)
    project(everything, LAGS - 1)


def shifted(value, steps):
    count = lax.axis_size(AXES)
    leading, last = (max(0, -steps), min(count, count - steps))
    return lax.ppermute(value, AXES, [(source, source + steps) for source in range(leading, last)])


def trade(value, groups):
    if len(groups[0]) == 1:
        return value
    return lax.all_to_all(value, AXES, 0, 0, axis_index_groups=groups)


def fan(value, copies):
    return pl.pallas_call(
        fan_kernel,
        out_shape=jax.ShapeDtypeStruct((copies,) + value.shape[1:], jnp.float32),
        in_specs=[pl.BlockSpec(memory_space=pltpu.VMEM)],
        out_specs=pl.BlockSpec(memory_space=pltpu.VMEM),
        compiler_params=pltpu.CompilerParams(vmem_limit_bytes=VMEM_LIMIT),
        name="add_and_repeat",
    )(value)


def across_cores(value):
    count = lax.axis_size("grp")
    return lax.ppermute(value, "grp", [(source, source ^ 1) for source in range(count)])


def spread_sum(keep, give):
    rows, depth = lax.axis_size("grp") // 2, lax.axis_size("span") // CHIPS_X

    def device(y, core, z, x):
        return ((y * 2 + core) * depth + z) * CHIPS_X + x

    planes = [
        [device(y, core, z, x) for y in range(rows) for x in range(CHIPS_X)] for core in range(2) for z in range(depth)
    ]
    columns = [
        [device(y, core, z, x) for z in range(depth)]
        for y in range(rows)
        for core in range(2)
        for x in range(CHIPS_X)
    ]
    plane = rows * CHIPS_X
    shares = trade(keep + across_cores(give), planes)
    shares = fan(shares, depth)
    mine = trade(fan(trade(shares, columns), plane), planes)
    return mine, across_cores(mine)


def averaged_blocks(record, edge):
    count = record.shape[0]
    smem, vmem = pl.BlockSpec(memory_space=pltpu.SMEM), pl.BlockSpec(memory_space=pltpu.VMEM)
    params = pltpu.CompilerParams(vmem_limit_bytes=VMEM_LIMIT)
    head, rear = pl.pallas_call(
        carve_kernel,
        out_shape=[jax.ShapeDtypeStruct((DOWN + 16, N), jnp.float32), jax.ShapeDtypeStruct((UP, N), jnp.float32)],
        in_specs=[pl.BlockSpec(memory_space=pltpu.HBM)],
        out_specs=[pl.BlockSpec(memory_space=pltpu.HBM)] * 2,
        scratch_shapes=[
            pltpu.VMEM((DOWN + 16 + UP, N), jnp.float32),
            pltpu.SemaphoreType.DMA((2 * CARVE,)),
            pltpu.SemaphoreType.DMA((2 * CARVE,)),
        ],
        compiler_params=pltpu.CompilerParams(vmem_limit_bytes=62 * 2**20),
        name="carve",
    )(record)
    down, up = shifted(head, -1), shifted(rear, 1)
    local, split = pl.pallas_call(
        local_kernel,
        out_shape=[
            jax.ShapeDtypeStruct((BLOCKS, N, N), jnp.float32),
            jax.ShapeDtypeStruct((count, 4 * N), jnp.bfloat16),
        ],
        in_specs=[smem, vmem],
        out_specs=[vmem, vmem],
        scratch_shapes=[pltpu.VMEM((LAGS * LAGS, N, N), jnp.float32)] * 3,
        compiler_params=params,
        cost_estimate=pl.CostEstimate(flops=4 * 10**9, bytes_accessed=8 * 2**20, transcendentals=0),
        name="local_products",
    )(edge, record)
    members = lax.axis_size("grp") // 2 * CHIPS_X
    side = jax.ShapeDtypeStruct((members, (GRAM_SIDE + CROSS_SIDE) * N // members, N), jnp.float32)
    keep, give = pl.pallas_call(
        halo_kernel,
        out_shape=[side, side],
        in_specs=[smem, vmem, vmem, vmem, vmem],
        out_specs=[vmem, vmem],
        scratch_shapes=[pltpu.VMEM((DOWN, 4 * N), jnp.bfloat16), pltpu.VMEM((UP, 4 * N), jnp.bfloat16)]
        + [pltpu.VMEM((2, GRAM_SIDE * N, N), jnp.float32), pltpu.VMEM((2, CROSS_SIDE * N, N), jnp.float32)],
        compiler_params=params,
        cost_estimate=pl.CostEstimate(flops=3 * 10**9, bytes_accessed=9 * 2**20, transcendentals=0),
        name="halo_products",
    )(edge, local, split, down, up)
    return spread_sum(keep, give)


def on_device(record):
    devices = lax.axis_size(AXES)
    last_row = record.shape[0] * devices - (LAGS - 1) * DELAY - 1
    index = lax.axis_index(AXES)
    edge = jnp.stack([index == 0, index == devices - 1, lax.axis_index("grp") % 2]).astype(jnp.int32)
    mine, other = averaged_blocks(record, edge)
    smem, vmem = pl.BlockSpec(memory_space=pltpu.SMEM), pl.BlockSpec(memory_space=pltpu.VMEM)
    square = jax.ShapeDtypeStruct((COLS, COLS), jnp.float32)
    return tuple(
        pl.pallas_call(
            functools.partial(tail_kernel, 1.0 / last_row),
            out_shape=[square, square],
            in_specs=[smem, vmem, vmem],
            out_specs=[vmem, vmem],
            scratch_shapes=[
                pltpu.VMEM((2, GRAM_SIDE * N, N), jnp.float32),
                pltpu.VMEM((2, CROSS_SIDE * N, N), jnp.float32),
                pltpu.VMEM((COLS, COLS), jnp.float32),
                pltpu.VMEM((COLS, COLS), jnp.float32),
                pltpu.VMEM((COLS, COLS), jnp.float32),
            ],
            compiler_params=pltpu.CompilerParams(vmem_limit_bytes=VMEM_LIMIT),
            name="factor_and_solve",
        )(edge, mine, other)
    )


def solution(mesh):
    placed = (P(AXES, None),)
    return jax.shard_map(on_device, mesh=mesh, in_specs=placed, out_specs=(P(), P()), check_vma=False)
```

```python
import functools

import jax
import jax.numpy as jnp
from jax import lax
from jax.experimental import pallas as pl
from jax.experimental.pallas import tpu as pltpu
from jax.sharding import PartitionSpec as P

LAGS = 4
DELAY = 1024
N = 128
COLS = LAGS * N
CUT = 608
DOWN, UP = DELAY + CUT, 2 * DELAY - CUT
AXES = ("grp", "span")
HIGHEST = lax.Precision.HIGHEST
VMEM_LIMIT = 24 * 2**20

PAIRS = [(i, j) for i in range(LAGS) for j in range(i, LAGS)]
GRAM = {pair: index for index, pair in enumerate(PAIRS)}
CROSS = {(i, j): len(PAIRS) + LAGS * i + j for i in range(LAGS) for j in range(LAGS)}
BLOCKS = len(GRAM) + len(CROSS)
GRAM_SIDE, CROSS_SIDE = len(GRAM) // 2, len(CROSS) // 2
CHIPS_X = 4
CARVE = 2
GROUP = 4


def exact(left, right, dims):
    return lax.dot_general(left, right, (dims, ((), ())), precision=HIGHEST, preferred_element_type=jnp.float32)


def rows_product(left, right):
    return lax.dot_general(left, right, (((0,), (0,)), ((), ())), preferred_element_type=jnp.float32)


def parts(value):
    high = value.astype(jnp.bfloat16)
    low = (value - high.astype(jnp.float32)).astype(jnp.bfloat16)
    return jnp.concatenate([high, low], 1)


def fold(value):
    return (value[:N, :N] + value[N:, :N]) + (value[:N, N:] + value[N:, N:])


def lag_products(left, right, zero_lag=False):
    first = rows_product(left, right[:, : 2 * N])
    same, back = fold(first[: 2 * N]), fold(first[2 * N :])
    ahead = None if zero_lag else fold(rows_product(left[:, : 2 * N], right[:, 2 * N :]))
    return same, back, ahead


def local_kernel(edge_ref, rec_ref, out_ref, split_ref, same_ref, back_ref, ahead_ref):
    count = rec_ref.shape[0]
    for q in range(LAGS):
        lo, hi = q * DELAY, (q + 1) * DELAY
        split_ref[lo:hi, : 2 * N] = parts(rec_ref[lo:hi, :])
        if q < LAGS - 1:
            following = rec_ref[lo + 1 : hi + 1, :]
        else:
            following = jnp.concatenate([rec_ref[lo + 1 : hi, :], jnp.zeros((1, N), jnp.float32)], 0)
        split_ref[lo:hi, 2 * N :] = parts(following)
    for q in range(LAGS):
        left = split_ref[q * DELAY : (q + 1) * DELAY, :]
        for d in range(LAGS - q):
            right = split_ref[(q + d) * DELAY : (q + d + 1) * DELAY, :]
            same, back, ahead = lag_products(left, right, d == 0)
            same_ref[LAGS * q + d] = same
            back_ref[LAGS * q + d] = back
            if d:
                ahead_ref[LAGS * q + d] = ahead
    first, last = edge_ref[0], edge_ref[1]

    def kept(q, m):
        if q < m:
            return (1 - first).astype(jnp.float32)
        if q > m:
            return (1 - last).astype(jnp.float32)
        return None

    def total(ref, d, m):
        value = None
        for q in range(LAGS - d):
            factor, term = kept(q, m), ref[LAGS * q + d]
            term = term if factor is None else term * factor
            value = term if value is None else value + term
        return value

    for i, j in PAIRS:
        d = j - i
        out_ref[GRAM[i, j]] = total(same_ref, d, i)
        out_ref[CROSS[j, i]] = total(back_ref, d, i)
        if d:
            out_ref[CROSS[i, j]] = total(ahead_ref, d, i)

    @pl.when(first + last > 0)
    def _():
        def wide(offset, steps):
            pieces = [rec_ref[offset + k * DELAY : offset + k * DELAY + 1, :] for k in range(steps)]
            pieces += [jnp.zeros((1, N), jnp.float32)] * (LAGS - steps)
            return jnp.concatenate(pieces, 1)

        start = wide(0, LAGS) * first.astype(jnp.float32)
        final = wide(DELAY - 1, LAGS) * last.astype(jnp.float32)
        after = wide(DELAY, LAGS - 1)
        blank = jnp.zeros((6, COLS), jnp.float32)
        ends = jnp.concatenate([start, final, blank], 0)
        steps = jnp.concatenate([jnp.zeros((1, COLS), jnp.float32), after, blank], 0)
        outer = ((0,), (0,))
        for i in range(LAGS):
            for j in range(LAGS):
                a, b = ends[:, i * N : (i + 1) * N], ends[:, j * N : (j + 1) * N]
                c = steps[:, j * N : (j + 1) * N]
                if j >= i:
                    out_ref[GRAM[i, j]] -= 0.5 * exact(a, b, outer)
                out_ref[CROSS[i, j]] -= exact(c, a, outer) if i >= j else exact(a, c, outer)


def carve_kernel(rec_ref, head_ref, rear_ref, held, in_sems, out_sems):
    count, parts_of = rec_ref.shape[0], CARVE
    pieces = []
    for ref, start in ((head_ref, 0), (rear_ref, count - rear_ref.shape[0])):
        size = ref.shape[0] // parts_of
        pieces += [(ref, start, p * size, size) for p in range(parts_of)]
    arrivals, departures, place = [], [], 0
    for n, (ref, start, offset, size) in enumerate(pieces):
        slot = held.at[place : place + size]
        arrivals.append(pltpu.make_async_copy(rec_ref.at[start + offset : start + offset + size], slot, in_sems.at[n]))
        departures.append(pltpu.make_async_copy(slot, ref.at[offset : offset + size], out_sems.at[n]))
        place += size
    for copy in arrivals:
        copy.start()
    for arrival, departure in zip(arrivals, departures):
        arrival.wait()
        departure.start()
    for copy in departures:
        copy.wait()


def fan_kernel(in_ref, out_ref):
    value = in_ref[0]
    for k in range(1, in_ref.shape[0]):
        value = value + in_ref[k]
    for k in range(out_ref.shape[0]):
        out_ref[k] = value


def halo_kernel(edge_ref, acc_ref, split_ref, down_ref, up_ref, keep_ref, give_ref, below, above, gram, cross):
    below[:, : 2 * N] = parts(down_ref[:DOWN, :])
    below[:, 2 * N :] = parts(down_ref[1 : DOWN + 1, :])
    above[:, : 2 * N] = parts(up_ref[...])
    own = split_ref[0:16, : 2 * N].astype(jnp.float32)[0:1]
    own = (own[:, :N] + own[:, N:]) * (1 - edge_ref[0]).astype(jnp.float32)
    above[:, 2 * N :] = parts(jnp.concatenate([up_ref[1:UP, :], own], 0))

    def own_rows(start, size):
        return split_ref[start : start + size, :]

    pairs = {
        1: [(own_rows(3 * DELAY, DELAY), below[:DELAY, :])],
        2: [(own_rows(2 * DELAY, DELAY), below[:DELAY, :]), (above[DELAY - CUT :, :], own_rows(DELAY, DELAY))],
        3: [
            (own_rows(DELAY, DELAY), below[:DELAY, :]),
            (above[DELAY - CUT :, :], own_rows(2 * DELAY, DELAY)),
            (own_rows(2 * DELAY, CUT), below[DELAY:, :]),
            (above[: DELAY - CUT, :], own_rows(DELAY + CUT, DELAY - CUT)),
        ],
    }
    core = edge_ref[2]

    def put(index, value):
        if index < len(GRAM):
            index, row = index // GRAM_SIDE, index % GRAM_SIDE * N
            gram[index ^ core, row : row + N] = value
        else:
            index -= len(GRAM)
            index, row = index // CROSS_SIDE, index % CROSS_SIDE * N
            cross[index ^ core, row : row + N] = value

    lastrow = lax.broadcasted_iota(jnp.int32, (16, N), 0) == 15
    entering = parts(jnp.where(lastrow, jnp.broadcast_to(down_ref[0:1, :], (16, N)), 0.0))
    count = LAGS * DELAY
    fix = fold(rows_product(entering, split_ref[count - 16 : count, : 2 * N]))
    for i in range(LAGS):
        put(GRAM[i, i], acc_ref[GRAM[i, i]])
        put(CROSS[i, i], acc_ref[CROSS[i, i]] + fix)
    for d in range(1, LAGS):
        stop = (LAGS - d) * DELAY
        same = None
        back = fold(rows_product(entering, below[DELAY - 16 : DELAY, : 2 * N])) if d == 1 else None
        ahead = fold(rows_product(split_ref[stop - 16 : stop, : 2 * N], entering))
        for left, right in pairs[d]:
            s, b, a = lag_products(left, right)
            same = s if same is None else same + s
            back = b if back is None else back + b
            ahead = ahead + a
        for i in range(LAGS - d):
            j = i + d
            put(GRAM[i, j], acc_ref[GRAM[i, j]] + same)
            put(CROSS[j, i], acc_ref[CROSS[j, i]] + back)
            put(CROSS[i, j], acc_ref[CROSS[i, j]] + ahead)
    members = keep_ref.shape[0]
    few, many = GRAM_SIDE * N // members, CROSS_SIDE * N // members
    for side, ref in enumerate((keep_ref, give_ref)):
        for m in range(members):
            ref[m, :few] = gram[side, m * few : (m + 1) * few]
            ref[m, few:] = cross[side, m * many : (m + 1) * many]


def lanes(value, j):
    return jnp.broadcast_to(value[:, j : j + 1], (value.shape[0], N))


def line(value, t, n):
    return jnp.broadcast_to(value[t : t + 1, :], (n, N))


def whole(ref, slot, row):
    return jnp.broadcast_to(ref[slot, row : row + 1, :], (8, N))


def three(value):
    high = value.astype(jnp.bfloat16)
    rest = value - high.astype(jnp.float32)
    mid = rest.astype(jnp.bfloat16)
    return high, mid, (rest - mid.astype(jnp.float32)).astype(jnp.bfloat16)


def stacked(left, right, left_dim, right_dim):
    (a, b, c), (x, y, z) = three(left), three(right)
    return lax.dot_general(
        jnp.concatenate([a, a, b, a, c, b], left_dim),
        jnp.concatenate([x, y, x, z, x, y], right_dim),
        (((left_dim,), (right_dim,)), ((), ())),
        preferred_element_type=jnp.float32,
    )


def factor(matrix, between, spread):
    sub = lax.broadcasted_iota(jnp.int32, (8, N), 0)
    lane = lax.broadcasted_iota(jnp.int32, (8, N), 1)
    rows = [matrix[r : r + 8] for r in range(0, N, 8)]
    uppers, inverses = [], []
    for k in range(len(rows)):
        first = 8 * k
        inside = (lane >= first) & (lane < first + 8)
        at = [lane == first + t for t in range(8)]
        cols = [lanes(rows[k], first + t) for t in range(8)]
        held = k % 2
        for u in range(8):
            spread[held, 8 * u : 8 * u + 8] = cols[u]
        spread[held, 64:72] = jnp.where(inside, 0.0, rows[k])
        corner = [[whole(spread, held, 8 * u + t) if u >= t else None for u in range(8)] for t in range(8)]
        top = [jnp.where(at[t], 1.0, whole(spread, held, 64 + t)) for t in range(8)]
        others = list(range(k + 1, k - k % GROUP + GROUP))
        below = {v: [lanes(rows[v], first + t) for t in range(8)] for v in others}
        for v in others:
            rows[v] = jnp.where(inside, 0.0, rows[v])
        pivots, both, diagonal = jnp.zeros((8, N), jnp.float32), jnp.zeros((8, N), jnp.float32), jnp.zeros((8, N), jnp.float32)
        for t in range(8):
            recip = 1.0 / corner[t][t]
            for u in range(t + 1, 8):
                mult = corner[t][u] * recip
                for w in range(u, 8):
                    corner[u][w] = corner[u][w] - mult * corner[t][w]
                top[u] = top[u] - mult * top[t]
            for v in others:
                mult = below[v][t] * recip
                for u in range(t + 1, 8):
                    below[v][u] = below[v][u] - mult * corner[t][u]
                rows[v] = rows[v] - mult * top[t]
            own = jnp.zeros((8, N), jnp.float32)
            for u in range(t, 8):
                own = jnp.where(at[u], corner[t][u], own)
            here = sub == t
            pivots = jnp.where(here, corner[t][t], pivots)
            both = jnp.where(here, top[t], both)
            diagonal = jnp.where(here, own, diagonal)
        root = lax.rsqrt(pivots)
        both = both * root
        uppers.append(jnp.where(lane >= first + 8, both, diagonal * root))
        inverses.append(jnp.where(lane < first + 8, both, 0.0))
        between()
        end = k + 1
        if end % GROUP == 0 and end < len(rows):
            upper = jnp.concatenate(uppers[-GROUP:], 0)
            columns = lax.broadcasted_iota(jnp.int32, upper.shape, 1)
            done = jnp.where(columns < 8 * end, jnp.concatenate(inverses[-GROUP:], 0), upper)
            update = stacked(upper, done, 0, 0)
            grouped = (lane >= 8 * (end - GROUP)) & (lane < 8 * end)
            for v in range(end, len(rows)):
                rows[v] = jnp.where(grouped, 0.0, rows[v]) - update[8 * v : 8 * v + 8]
    return jnp.concatenate(uppers, 0), jnp.concatenate(inverses, 0)


def tail_kernel(scale, edge_ref, mine_ref, other_ref, tri_ref, op_ref, gram, cross, work, inv, left, spread):
    core = edge_ref[2]
    few = gram.shape[1] // mine_ref.shape[0]
    many = cross.shape[1] // mine_ref.shape[0]
    for side, ref in ((core, mine_ref), (1 - core, other_ref)):
        for m in range(ref.shape[0]):
            gram[side, m * few : (m + 1) * few] = ref[m, :few] * scale
            cross[side, m * many : (m + 1) * many] = ref[m, few:] * scale
    factor_and_solve(gram, cross, tri_ref, op_ref, inv, work, left, spread)


def factor_and_solve(gram, cross, tri_ref, op_ref, inv_ref, work, left, spread):
    def block(k):
        return slice(k * N, (k + 1) * N)

    zero = jnp.zeros((N, N), jnp.float32)
    for k in range(LAGS):
        for j in range(k):
            tri_ref[block(k), block(j)] = zero
            inv_ref[block(j), block(k)] = zero
            work[block(k), block(j)] = zero
    for (i, j), index in GRAM.items():
        row = index % GRAM_SIDE * N
        work[block(i), block(j)] = gram[index // GRAM_SIDE, row : row + N]
    waiting = []

    def between():
        if waiting:
            waiting.pop(0)()

    def fetch(i, j):
        index = CROSS[i, j] - len(GRAM)
        row = index % CROSS_SIDE * N
        value = cross[index // CROSS_SIDE, row : row + N]
        left[block(i), block(j)] = value.T if i >= j else value

    def solve_side(k, inverse, target, source, columns):
        target[block(k), columns] = stacked(inverse, source[block(k), columns], 1, 0)

    def update(k, i, target, source, columns):
        target[block(i), columns] -= stacked(tri_ref[block(k), block(i)], source[block(k), columns], 0, 0)

    def project(rows, j):
        known = slice(0, (j + 1) * N)
        op_ref[rows, block(j)] = stacked(left[rows, known], inv_ref[block(j), known], 1, 1)

    def later(function, *args):
        waiting.append(functools.partial(function, *args))

    for i in range(LAGS):
        for j in range(LAGS):
            later(fetch, i, j)
    everything = slice(0, COLS)
    for k in range(LAGS):
        upper, inverse = factor(work[block(k), block(k)], between, spread)
        while waiting:
            between()
        tri_ref[block(k), block(k)] = upper
        inv_ref[block(k), block(k)] = inverse
        if k + 1 < LAGS:
            solve_side(k, inverse, tri_ref, work, block(k + 1))
            update(k, k + 1, work, tri_ref, block(k + 1))
        if k + 2 < LAGS:
            later(solve_side, k, inverse, tri_ref, work, slice((k + 2) * N, COLS))
        if k:
            later(solve_side, k, inverse, inv_ref, work, slice(0, k * N))
        later(solve_side, k, inverse, left, left, everything)
        for i in range(k + 1, LAGS):
            start = max(i, k + 2) * N
            if start < COLS:
                later(update, k, i, work, tri_ref, slice(start, COLS))
            later(update, k, i, work, inv_ref, slice(0, (k + 1) * N))
            later(update, k, i, left, left, everything)
        if k == LAGS - 2:
            for j in range(LAGS - 1):
                later(project, slice(0, (LAGS - 1) * N), j)
    while waiting:
        between()
    for j in range(LAGS - 1):
        project(block(LAGS - 1), j)
    project(everything, LAGS - 1)


def shifted(value, steps):
    count = lax.axis_size(AXES)
    leading, last = (max(0, -steps), min(count, count - steps))
    return lax.ppermute(value, AXES, [(source, source + steps) for source in range(leading, last)])


def trade(value, groups):
    if len(groups[0]) == 1:
        return value
    return lax.all_to_all(value, AXES, 0, 0, axis_index_groups=groups)


def fan(value, copies):
    return pl.pallas_call(
        fan_kernel,
        out_shape=jax.ShapeDtypeStruct((copies,) + value.shape[1:], jnp.float32),
        in_specs=[pl.BlockSpec(memory_space=pltpu.VMEM)],
        out_specs=pl.BlockSpec(memory_space=pltpu.VMEM),
        compiler_params=pltpu.CompilerParams(vmem_limit_bytes=VMEM_LIMIT),
        name="add_and_repeat",
    )(value)


def across_cores(value):
    count = lax.axis_size("grp")
    return lax.ppermute(value, "grp", [(source, source ^ 1) for source in range(count)])


def spread_sum(keep, give):
    rows, depth = lax.axis_size("grp") // 2, lax.axis_size("span") // CHIPS_X

    def device(y, core, z, x):
        return ((y * 2 + core) * depth + z) * CHIPS_X + x

    planes = [
        [device(y, core, z, x) for y in range(rows) for x in range(CHIPS_X)] for core in range(2) for z in range(depth)
    ]
    columns = [
        [device(y, core, z, x) for z in range(depth)]
        for y in range(rows)
        for core in range(2)
        for x in range(CHIPS_X)
    ]
    plane = rows * CHIPS_X
    shares = trade(keep + across_cores(give), planes)
    shares = fan(shares, depth)
    mine = trade(fan(trade(shares, columns), plane), planes)
    return mine, across_cores(mine)


def averaged_blocks(record, edge):
    count = record.shape[0]
    smem, vmem = pl.BlockSpec(memory_space=pltpu.SMEM), pl.BlockSpec(memory_space=pltpu.VMEM)
    params = pltpu.CompilerParams(vmem_limit_bytes=VMEM_LIMIT)
    head, rear = pl.pallas_call(
        carve_kernel,
        out_shape=[jax.ShapeDtypeStruct((DOWN + 16, N), jnp.float32), jax.ShapeDtypeStruct((UP, N), jnp.float32)],
        in_specs=[pl.BlockSpec(memory_space=pltpu.HBM)],
        out_specs=[pl.BlockSpec(memory_space=pltpu.HBM)] * 2,
        scratch_shapes=[
            pltpu.VMEM((DOWN + 16 + UP, N), jnp.float32),
            pltpu.SemaphoreType.DMA((2 * CARVE,)),
            pltpu.SemaphoreType.DMA((2 * CARVE,)),
        ],
        compiler_params=pltpu.CompilerParams(vmem_limit_bytes=62 * 2**20),
        name="carve",
    )(record)
    down, up = shifted(head, -1), shifted(rear, 1)
    local, split = pl.pallas_call(
        local_kernel,
        out_shape=[
            jax.ShapeDtypeStruct((BLOCKS, N, N), jnp.float32),
            jax.ShapeDtypeStruct((count, 4 * N), jnp.bfloat16),
        ],
        in_specs=[smem, vmem],
        out_specs=[vmem, vmem],
        scratch_shapes=[pltpu.VMEM((LAGS * LAGS, N, N), jnp.float32)] * 3,
        compiler_params=params,
        cost_estimate=pl.CostEstimate(flops=4 * 10**9, bytes_accessed=8 * 2**20, transcendentals=0),
        name="local_products",
    )(edge, record)
    members = lax.axis_size("grp") // 2 * CHIPS_X
    side = jax.ShapeDtypeStruct((members, (GRAM_SIDE + CROSS_SIDE) * N // members, N), jnp.float32)
    keep, give = pl.pallas_call(
        halo_kernel,
        out_shape=[side, side],
        in_specs=[smem, vmem, vmem, vmem, vmem],
        out_specs=[vmem, vmem],
        scratch_shapes=[pltpu.VMEM((DOWN, 4 * N), jnp.bfloat16), pltpu.VMEM((UP, 4 * N), jnp.bfloat16)]
        + [pltpu.VMEM((2, GRAM_SIDE * N, N), jnp.float32), pltpu.VMEM((2, CROSS_SIDE * N, N), jnp.float32)],
        compiler_params=params,
        cost_estimate=pl.CostEstimate(flops=3 * 10**9, bytes_accessed=9 * 2**20, transcendentals=0),
        name="halo_products",
    )(edge, local, split, down, up)
    return spread_sum(keep, give)


def on_device(record):
    devices = lax.axis_size(AXES)
    last_row = record.shape[0] * devices - (LAGS - 1) * DELAY - 1
    index = lax.axis_index(AXES)
    edge = jnp.stack([index == 0, index == devices - 1, lax.axis_index("grp") % 2]).astype(jnp.int32)
    mine, other = averaged_blocks(record, edge)
    smem, vmem = pl.BlockSpec(memory_space=pltpu.SMEM), pl.BlockSpec(memory_space=pltpu.VMEM)
    square = jax.ShapeDtypeStruct((COLS, COLS), jnp.float32)
    return tuple(
        pl.pallas_call(
            functools.partial(tail_kernel, 1.0 / last_row),
            out_shape=[square, square],
            in_specs=[smem, vmem, vmem],
            out_specs=[vmem, vmem],
            scratch_shapes=[
                pltpu.VMEM((2, GRAM_SIDE * N, N), jnp.float32),
                pltpu.VMEM((2, CROSS_SIDE * N, N), jnp.float32),
                pltpu.VMEM((COLS, COLS), jnp.float32),
                pltpu.VMEM((COLS, COLS), jnp.float32),
                pltpu.VMEM((COLS, COLS), jnp.float32),
                pltpu.VMEM((2, 72, N), jnp.float32),
            ],
            compiler_params=pltpu.CompilerParams(vmem_limit_bytes=VMEM_LIMIT),
            name="factor_and_solve",
        )(edge, mine, other)
    )


def solution(mesh):
    placed = (P(AXES, None),)
    return jax.shard_map(on_device, mesh=mesh, in_specs=placed, out_specs=(P(), P()), check_vma=False)
```

```python
import functools

import jax
import jax.numpy as jnp
from jax import lax
from jax.experimental import pallas as pl
from jax.experimental.pallas import tpu as pltpu
from jax.sharding import PartitionSpec as P

LAGS = 4
DELAY = 1024
N = 128
COLS = LAGS * N
CUT = 608
DOWN, UP = DELAY + CUT, 2 * DELAY - CUT
AXES = ("grp", "span")
HIGHEST = lax.Precision.HIGHEST
VMEM_LIMIT = 24 * 2**20

PAIRS = [(i, j) for i in range(LAGS) for j in range(i, LAGS)]
GRAM = {pair: index for index, pair in enumerate(PAIRS)}
CROSS = {(i, j): len(PAIRS) + LAGS * i + j for i in range(LAGS) for j in range(LAGS)}
BLOCKS = len(GRAM) + len(CROSS)
GRAM_SIDE, CROSS_SIDE = len(GRAM) // 2, len(CROSS) // 2
CHIPS_X = 4
CARVE = 2
GROUP = 8


def exact(left, right, dims):
    return lax.dot_general(left, right, (dims, ((), ())), precision=HIGHEST, preferred_element_type=jnp.float32)


def rows_product(left, right):
    return lax.dot_general(left, right, (((0,), (0,)), ((), ())), preferred_element_type=jnp.float32)


def parts(value):
    high = value.astype(jnp.bfloat16)
    low = (value - high.astype(jnp.float32)).astype(jnp.bfloat16)
    return jnp.concatenate([high, low], 1)


def fold(value):
    return (value[:N, :N] + value[N:, :N]) + (value[:N, N:] + value[N:, N:])


def lag_products(left, right, zero_lag=False):
    first = rows_product(left, right[:, : 2 * N])
    same, back = fold(first[: 2 * N]), fold(first[2 * N :])
    ahead = None if zero_lag else fold(rows_product(left[:, : 2 * N], right[:, 2 * N :]))
    return same, back, ahead


def local_kernel(edge_ref, rec_ref, out_ref, split_ref, same_ref, back_ref, ahead_ref):
    count = rec_ref.shape[0]
    for q in range(LAGS):
        lo, hi = q * DELAY, (q + 1) * DELAY
        split_ref[lo:hi, : 2 * N] = parts(rec_ref[lo:hi, :])
        if q < LAGS - 1:
            following = rec_ref[lo + 1 : hi + 1, :]
        else:
            following = jnp.concatenate([rec_ref[lo + 1 : hi, :], jnp.zeros((1, N), jnp.float32)], 0)
        split_ref[lo:hi, 2 * N :] = parts(following)
    for q in range(LAGS):
        left = split_ref[q * DELAY : (q + 1) * DELAY, :]
        for d in range(LAGS - q):
            right = split_ref[(q + d) * DELAY : (q + d + 1) * DELAY, :]
            same, back, ahead = lag_products(left, right, d == 0)
            same_ref[LAGS * q + d] = same
            back_ref[LAGS * q + d] = back
            if d:
                ahead_ref[LAGS * q + d] = ahead
    first, last = edge_ref[0], edge_ref[1]

    def kept(q, m):
        if q < m:
            return (1 - first).astype(jnp.float32)
        if q > m:
            return (1 - last).astype(jnp.float32)
        return None

    def total(ref, d, m):
        value = None
        for q in range(LAGS - d):
            factor, term = kept(q, m), ref[LAGS * q + d]
            term = term if factor is None else term * factor
            value = term if value is None else value + term
        return value

    for i, j in PAIRS:
        d = j - i
        out_ref[GRAM[i, j]] = total(same_ref, d, i)
        out_ref[CROSS[j, i]] = total(back_ref, d, i)
        if d:
            out_ref[CROSS[i, j]] = total(ahead_ref, d, i)

    @pl.when(first + last > 0)
    def _():
        def wide(offset, steps):
            pieces = [rec_ref[offset + k * DELAY : offset + k * DELAY + 1, :] for k in range(steps)]
            pieces += [jnp.zeros((1, N), jnp.float32)] * (LAGS - steps)
            return jnp.concatenate(pieces, 1)

        start = wide(0, LAGS) * first.astype(jnp.float32)
        final = wide(DELAY - 1, LAGS) * last.astype(jnp.float32)
        after = wide(DELAY, LAGS - 1)
        blank = jnp.zeros((6, COLS), jnp.float32)
        ends = jnp.concatenate([start, final, blank], 0)
        steps = jnp.concatenate([jnp.zeros((1, COLS), jnp.float32), after, blank], 0)
        outer = ((0,), (0,))
        for i in range(LAGS):
            for j in range(LAGS):
                a, b = ends[:, i * N : (i + 1) * N], ends[:, j * N : (j + 1) * N]
                c = steps[:, j * N : (j + 1) * N]
                if j >= i:
                    out_ref[GRAM[i, j]] -= 0.5 * exact(a, b, outer)
                out_ref[CROSS[i, j]] -= exact(c, a, outer) if i >= j else exact(a, c, outer)


def carve_kernel(rec_ref, head_ref, rear_ref, held, in_sems, out_sems):
    count, parts_of = rec_ref.shape[0], CARVE
    pieces = []
    for ref, start in ((head_ref, 0), (rear_ref, count - rear_ref.shape[0])):
        size = ref.shape[0] // parts_of
        pieces += [(ref, start, p * size, size) for p in range(parts_of)]
    arrivals, departures, place = [], [], 0
    for n, (ref, start, offset, size) in enumerate(pieces):
        slot = held.at[place : place + size]
        arrivals.append(pltpu.make_async_copy(rec_ref.at[start + offset : start + offset + size], slot, in_sems.at[n]))
        departures.append(pltpu.make_async_copy(slot, ref.at[offset : offset + size], out_sems.at[n]))
        place += size
    for copy in arrivals:
        copy.start()
    for arrival, departure in zip(arrivals, departures):
        arrival.wait()
        departure.start()
    for copy in departures:
        copy.wait()


def fan_kernel(in_ref, out_ref):
    value = in_ref[0]
    for k in range(1, in_ref.shape[0]):
        value = value + in_ref[k]
    for k in range(out_ref.shape[0]):
        out_ref[k] = value


def halo_kernel(edge_ref, acc_ref, split_ref, down_ref, up_ref, keep_ref, give_ref, below, above, gram, cross):
    below[:, : 2 * N] = parts(down_ref[:DOWN, :])
    below[:, 2 * N :] = parts(down_ref[1 : DOWN + 1, :])
    above[:, : 2 * N] = parts(up_ref[...])
    own = split_ref[0:16, : 2 * N].astype(jnp.float32)[0:1]
    own = (own[:, :N] + own[:, N:]) * (1 - edge_ref[0]).astype(jnp.float32)
    above[:, 2 * N :] = parts(jnp.concatenate([up_ref[1:UP, :], own], 0))

    def own_rows(start, size):
        return split_ref[start : start + size, :]

    pairs = {
        1: [(own_rows(3 * DELAY, DELAY), below[:DELAY, :])],
        2: [(own_rows(2 * DELAY, DELAY), below[:DELAY, :]), (above[DELAY - CUT :, :], own_rows(DELAY, DELAY))],
        3: [
            (own_rows(DELAY, DELAY), below[:DELAY, :]),
            (above[DELAY - CUT :, :], own_rows(2 * DELAY, DELAY)),
            (own_rows(2 * DELAY, CUT), below[DELAY:, :]),
            (above[: DELAY - CUT, :], own_rows(DELAY + CUT, DELAY - CUT)),
        ],
    }
    core = edge_ref[2]

    def put(index, value):
        if index < len(GRAM):
            index, row = index // GRAM_SIDE, index % GRAM_SIDE * N
            gram[index ^ core, row : row + N] = value
        else:
            index -= len(GRAM)
            index, row = index // CROSS_SIDE, index % CROSS_SIDE * N
            cross[index ^ core, row : row + N] = value

    lastrow = lax.broadcasted_iota(jnp.int32, (16, N), 0) == 15
    entering = parts(jnp.where(lastrow, jnp.broadcast_to(down_ref[0:1, :], (16, N)), 0.0))
    count = LAGS * DELAY
    fix = fold(rows_product(entering, split_ref[count - 16 : count, : 2 * N]))
    for i in range(LAGS):
        put(GRAM[i, i], acc_ref[GRAM[i, i]])
        put(CROSS[i, i], acc_ref[CROSS[i, i]] + fix)
    for d in range(1, LAGS):
        stop = (LAGS - d) * DELAY
        same = None
        back = fold(rows_product(entering, below[DELAY - 16 : DELAY, : 2 * N])) if d == 1 else None
        ahead = fold(rows_product(split_ref[stop - 16 : stop, : 2 * N], entering))
        for left, right in pairs[d]:
            s, b, a = lag_products(left, right)
            same = s if same is None else same + s
            back = b if back is None else back + b
            ahead = ahead + a
        for i in range(LAGS - d):
            j = i + d
            put(GRAM[i, j], acc_ref[GRAM[i, j]] + same)
            put(CROSS[j, i], acc_ref[CROSS[j, i]] + back)
            put(CROSS[i, j], acc_ref[CROSS[i, j]] + ahead)
    members = keep_ref.shape[0]
    few, many = GRAM_SIDE * N // members, CROSS_SIDE * N // members
    for side, ref in enumerate((keep_ref, give_ref)):
        for m in range(members):
            ref[m, :few] = gram[side, m * few : (m + 1) * few]
            ref[m, few:] = cross[side, m * many : (m + 1) * many]


def lanes(value, j):
    return jnp.broadcast_to(value[:, j : j + 1], (value.shape[0], N))


def line(value, t, n):
    return jnp.broadcast_to(value[t : t + 1, :], (n, N))


def whole(ref, slot, row):
    return jnp.broadcast_to(ref[slot, row : row + 1, :], (8, N))


def three(value):
    high = value.astype(jnp.bfloat16)
    rest = value - high.astype(jnp.float32)
    mid = rest.astype(jnp.bfloat16)
    return high, mid, (rest - mid.astype(jnp.float32)).astype(jnp.bfloat16)


def stacked(left, right, left_dim, right_dim):
    (a, b, c), (x, y, z) = three(left), three(right)
    return lax.dot_general(
        jnp.concatenate([a, a, b, a, c, b], left_dim),
        jnp.concatenate([x, y, x, z, x, y], right_dim),
        (((left_dim,), (right_dim,)), ((), ())),
        preferred_element_type=jnp.float32,
    )


def factor(matrix, between, spread):
    sub = lax.broadcasted_iota(jnp.int32, (8, N), 0)
    lane = lax.broadcasted_iota(jnp.int32, (8, N), 1)
    rows = [matrix[r : r + 8] for r in range(0, N, 8)]
    uppers, inverses = [], []
    for k in range(len(rows)):
        first = 8 * k
        inside = (lane >= first) & (lane < first + 8)
        at = [lane == first + t for t in range(8)]
        cols = [lanes(rows[k], first + t) for t in range(8)]
        held = k % 2
        for u in range(8):
            spread[held, 8 * u : 8 * u + 8] = cols[u]
        spread[held, 64:72] = jnp.where(inside, 0.0, rows[k])
        corner = [[whole(spread, held, 8 * u + t) if u >= t else None for u in range(8)] for t in range(8)]
        top = [jnp.where(at[t], 1.0, whole(spread, held, 64 + t)) for t in range(8)]
        others = list(range(k + 1, k - k % GROUP + GROUP))
        below = {v: [lanes(rows[v], first + t) for t in range(8)] for v in others}
        for v in others:
            rows[v] = jnp.where(inside, 0.0, rows[v])
        pivots, both, diagonal = jnp.zeros((8, N), jnp.float32), jnp.zeros((8, N), jnp.float32), jnp.zeros((8, N), jnp.float32)
        for t in range(8):
            recip = 1.0 / corner[t][t]
            for u in range(t + 1, 8):
                mult = corner[t][u] * recip
                for w in range(u, 8):
                    corner[u][w] = corner[u][w] - mult * corner[t][w]
                top[u] = top[u] - mult * top[t]
            for v in others:
                mult = below[v][t] * recip
                for u in range(t + 1, 8):
                    below[v][u] = below[v][u] - mult * corner[t][u]
                rows[v] = rows[v] - mult * top[t]
            own = jnp.zeros((8, N), jnp.float32)
            for u in range(t, 8):
                own = jnp.where(at[u], corner[t][u], own)
            here = sub == t
            pivots = jnp.where(here, corner[t][t], pivots)
            both = jnp.where(here, top[t], both)
            diagonal = jnp.where(here, own, diagonal)
        root = lax.rsqrt(pivots)
        both = both * root
        uppers.append(jnp.where(lane >= first + 8, both, diagonal * root))
        inverses.append(jnp.where(lane < first + 8, both, 0.0))
        between()
        end = k + 1
        if end % GROUP == 0 and end < len(rows):
            upper = jnp.concatenate(uppers[-GROUP:], 0)
            columns = lax.broadcasted_iota(jnp.int32, upper.shape, 1)
            done = jnp.where(columns < 8 * end, jnp.concatenate(inverses[-GROUP:], 0), upper)
            update = stacked(upper, done, 0, 0)
            grouped = (lane >= 8 * (end - GROUP)) & (lane < 8 * end)
            for v in range(end, len(rows)):
                rows[v] = jnp.where(grouped, 0.0, rows[v]) - update[8 * v : 8 * v + 8]
    return jnp.concatenate(uppers, 0), jnp.concatenate(inverses, 0)


def tail_kernel(scale, edge_ref, mine_ref, other_ref, tri_ref, op_ref, gram, cross, work, inv, left, spread):
    core = edge_ref[2]
    few = gram.shape[1] // mine_ref.shape[0]
    many = cross.shape[1] // mine_ref.shape[0]
    for side, ref in ((core, mine_ref), (1 - core, other_ref)):
        for m in range(ref.shape[0]):
            gram[side, m * few : (m + 1) * few] = ref[m, :few] * scale
            cross[side, m * many : (m + 1) * many] = ref[m, few:] * scale
    factor_and_solve(gram, cross, tri_ref, op_ref, inv, work, left, spread)


def factor_and_solve(gram, cross, tri_ref, op_ref, inv_ref, work, left, spread):
    def block(k):
        return slice(k * N, (k + 1) * N)

    zero = jnp.zeros((N, N), jnp.float32)
    for k in range(LAGS):
        for j in range(k):
            tri_ref[block(k), block(j)] = zero
            inv_ref[block(j), block(k)] = zero
            work[block(k), block(j)] = zero
    for (i, j), index in GRAM.items():
        row = index % GRAM_SIDE * N
        work[block(i), block(j)] = gram[index // GRAM_SIDE, row : row + N]
    waiting = []

    def between():
        if waiting:
            waiting.pop(0)()

    def fetch(i, j):
        index = CROSS[i, j] - len(GRAM)
        row = index % CROSS_SIDE * N
        value = cross[index // CROSS_SIDE, row : row + N]
        left[block(i), block(j)] = value.T if i >= j else value

    def solve_side(k, inverse, target, source, columns):
        target[block(k), columns] = stacked(inverse, source[block(k), columns], 1, 0)

    def update(k, i, *triples):
        right = jnp.concatenate([source[block(k), columns] for _, source, columns in triples], 1)
        change, start = stacked(tri_ref[block(k), block(i)].T, right, 1, 0), 0
        for target, _, columns in triples:
            stop = start + columns.stop - columns.start
            target[block(i), columns] -= change[:, start:stop]
            start = stop

    def project(j):
        known = slice(0, (j + 1) * N)
        op_ref[:, block(j)] = stacked(left[:, known], inv_ref[block(j), known], 1, 1)

    def project_last():
        known = slice(0, (LAGS - 1) * N)
        op_ref[:, block(LAGS - 1)] = left[:, block(LAGS - 1)] + stacked(left[:, known], work[block(LAGS - 1), known], 1, 1)

    def later(function, *args):
        waiting.append(functools.partial(function, *args))

    for i in range(LAGS):
        for j in range(LAGS):
            later(fetch, i, j)
    everything = slice(0, COLS)
    for k in range(LAGS):
        upper, inverse = factor(work[block(k), block(k)], between, spread)
        while waiting:
            between()
        tri_ref[block(k), block(k)] = upper
        if k == LAGS - 1:
            break
        inv_ref[block(k), block(k)] = inverse
        solve_side(k, inverse, tri_ref, work, block(k + 1))
        update(k, k + 1, (work, tri_ref, block(k + 1)))
        if k + 2 < LAGS:
            later(solve_side, k, inverse, tri_ref, work, slice((k + 2) * N, COLS))
        if k:
            later(solve_side, k, inverse, inv_ref, work, slice(0, k * N))
        later(solve_side, k, inverse, left, left, everything)
        for i in range(k + 1, LAGS):
            triples = [(work, inv_ref, slice(0, (k + 1) * N)), (left, left, everything)]
            start = max(i, k + 2) * N
            if start < COLS:
                triples.append((work, tri_ref, slice(start, COLS)))
            later(update, k, i, *triples)
        if k == LAGS - 2:
            for j in range(LAGS - 1):
                later(project, j)
            later(project_last)
    op_ref[:, block(k)] = stacked(op_ref[:, block(k)], inverse, 1, 1)
    op_ref[block(k), :] = stacked(inverse, op_ref[block(k), :], 1, 0)


def shifted(value, steps):
    count = lax.axis_size(AXES)
    leading, last = (max(0, -steps), min(count, count - steps))
    return lax.ppermute(value, AXES, [(source, source + steps) for source in range(leading, last)])


def trade(value, groups):
    if len(groups[0]) == 1:
        return value
    return lax.all_to_all(value, AXES, 0, 0, axis_index_groups=groups)


def fan(value, copies):
    return pl.pallas_call(
        fan_kernel,
        out_shape=jax.ShapeDtypeStruct((copies,) + value.shape[1:], jnp.float32),
        in_specs=[pl.BlockSpec(memory_space=pltpu.VMEM)],
        out_specs=pl.BlockSpec(memory_space=pltpu.VMEM),
        compiler_params=pltpu.CompilerParams(vmem_limit_bytes=VMEM_LIMIT),
        name="add_and_repeat",
    )(value)


def across_cores(value):
    count = lax.axis_size("grp")
    return lax.ppermute(value, "grp", [(source, source ^ 1) for source in range(count)])


def spread_sum(keep, give):
    rows, depth = lax.axis_size("grp") // 2, lax.axis_size("span") // CHIPS_X

    def device(y, core, z, x):
        return ((y * 2 + core) * depth + z) * CHIPS_X + x

    planes = [
        [device(y, core, z, x) for y in range(rows) for x in range(CHIPS_X)] for core in range(2) for z in range(depth)
    ]
    columns = [
        [device(y, core, z, x) for z in range(depth)]
        for y in range(rows)
        for core in range(2)
        for x in range(CHIPS_X)
    ]
    plane = rows * CHIPS_X
    shares = trade(keep + across_cores(give), planes)
    shares = fan(shares, depth)
    mine = trade(fan(trade(shares, columns), plane), planes)
    return mine, across_cores(mine)


def averaged_blocks(record, edge):
    count = record.shape[0]
    smem, vmem = pl.BlockSpec(memory_space=pltpu.SMEM), pl.BlockSpec(memory_space=pltpu.VMEM)
    params = pltpu.CompilerParams(vmem_limit_bytes=VMEM_LIMIT)
    head, rear = pl.pallas_call(
        carve_kernel,
        out_shape=[jax.ShapeDtypeStruct((DOWN + 16, N), jnp.float32), jax.ShapeDtypeStruct((UP, N), jnp.float32)],
        in_specs=[pl.BlockSpec(memory_space=pltpu.HBM)],
        out_specs=[pl.BlockSpec(memory_space=pltpu.HBM)] * 2,
        scratch_shapes=[
            pltpu.VMEM((DOWN + 16 + UP, N), jnp.float32),
            pltpu.SemaphoreType.DMA((2 * CARVE,)),
            pltpu.SemaphoreType.DMA((2 * CARVE,)),
        ],
        compiler_params=pltpu.CompilerParams(vmem_limit_bytes=62 * 2**20),
        name="carve",
    )(record)
    down, up = shifted(head, -1), shifted(rear, 1)
    local, split = pl.pallas_call(
        local_kernel,
        out_shape=[
            jax.ShapeDtypeStruct((BLOCKS, N, N), jnp.float32),
            jax.ShapeDtypeStruct((count, 4 * N), jnp.bfloat16),
        ],
        in_specs=[smem, vmem],
        out_specs=[vmem, vmem],
        scratch_shapes=[pltpu.VMEM((LAGS * LAGS, N, N), jnp.float32)] * 3,
        compiler_params=params,
        cost_estimate=pl.CostEstimate(flops=4 * 10**9, bytes_accessed=8 * 2**20, transcendentals=0),
        name="local_products",
    )(edge, record)
    members = lax.axis_size("grp") // 2 * CHIPS_X
    side = jax.ShapeDtypeStruct((members, (GRAM_SIDE + CROSS_SIDE) * N // members, N), jnp.float32)
    keep, give = pl.pallas_call(
        halo_kernel,
        out_shape=[side, side],
        in_specs=[smem, vmem, vmem, vmem, vmem],
        out_specs=[vmem, vmem],
        scratch_shapes=[pltpu.VMEM((DOWN, 4 * N), jnp.bfloat16), pltpu.VMEM((UP, 4 * N), jnp.bfloat16)]
        + [pltpu.VMEM((2, GRAM_SIDE * N, N), jnp.float32), pltpu.VMEM((2, CROSS_SIDE * N, N), jnp.float32)],
        compiler_params=params,
        cost_estimate=pl.CostEstimate(flops=3 * 10**9, bytes_accessed=9 * 2**20, transcendentals=0),
        name="halo_products",
    )(edge, local, split, down, up)
    return spread_sum(keep, give)


def on_device(record):
    devices = lax.axis_size(AXES)
    last_row = record.shape[0] * devices - (LAGS - 1) * DELAY - 1
    index = lax.axis_index(AXES)
    edge = jnp.stack([index == 0, index == devices - 1, lax.axis_index("grp") % 2]).astype(jnp.int32)
    mine, other = averaged_blocks(record, edge)
    smem, vmem = pl.BlockSpec(memory_space=pltpu.SMEM), pl.BlockSpec(memory_space=pltpu.VMEM)
    square = jax.ShapeDtypeStruct((COLS, COLS), jnp.float32)
    return tuple(
        pl.pallas_call(
            functools.partial(tail_kernel, 1.0 / last_row),
            out_shape=[square, square],
            in_specs=[smem, vmem, vmem],
            out_specs=[vmem, vmem],
            scratch_shapes=[
                pltpu.VMEM((2, GRAM_SIDE * N, N), jnp.float32),
                pltpu.VMEM((2, CROSS_SIDE * N, N), jnp.float32),
                pltpu.VMEM((COLS, COLS), jnp.float32),
                pltpu.VMEM((COLS, COLS), jnp.float32),
                pltpu.VMEM((COLS, COLS), jnp.float32),
                pltpu.VMEM((2, 72, N), jnp.float32),
            ],
            compiler_params=pltpu.CompilerParams(vmem_limit_bytes=VMEM_LIMIT),
            name="factor_and_solve",
        )(edge, mine, other)
    )


def solution(mesh):
    placed = (P(AXES, None),)
    return jax.shard_map(on_device, mesh=mesh, in_specs=placed, out_specs=(P(), P()), check_vma=False)
```
